256 devices in a mesh: gx: 64 (over x_lo, y, z), col: 4 (over x_hi, core).
Axes of the slice: x: 4 (x_hi: 2, x_lo: 2; x = x_hi * 2 + x_lo), y: 4, z: 8, core: 2. Of those that a mesh axis runs over, the one named last changes fastest.
Arguments:
- state: bfloat16 [128, 64, 128, 128], P(None, 'gx', 'col'), may hold values from -6 to 6
- target: bfloat16 [128, 64, 128, 128], P(None, 'gx', 'col'), may hold values from -6 to 6
- spectral_weight: bfloat16 [2, 128, 16, 512, 128], P(None, None, None, ('gx', 'col')), may hold values from -0.375 to 0.375
- direction_weight: bfloat16 [2, 128, 16, 512, 128], P(None, None, None, ('gx', 'col')), may hold values from -0.375 to 0.375
- inner_weight: bfloat16 [128, 512], replicated, may hold values from -0.5 to 0.5
- outer_weight: bfloat16 [512, 128], replicated, may hold values from -0.25 to 0.25
Outputs:
- gradient: bfloat16 [2, 128, 16, 512, 128], P(None, None, None, ('gx', 'col'))
- curvature: bfloat16 [2, 128, 16, 512, 128], P(None, None, None, ('gx', 'col'))
The draws below stay inside these ranges and needn't reach their ends.
All inputs are finite; a program needn't handle non-finite values.
Results may differ from the reference program's by a relative error of at most 0.0045.
Values sent between devices are 32-bit elements; how exact they have to be, the bound alone decides.
No kernel may reach another device: no remote copies, remote signals or barrier semaphores. Data moves between devices by JAX's collectives and lax.ppermute only.
A program may use at most 128 MiB of HBM per device.

```python
import math
import jax
import jax.numpy as jnp
from jax import lax

C = 128
FF = 512
NY = 128
NZ = 128
MX = 16
MY = 32
MZ = 16
NX = 64
MYZ = 512


def steps_of(key, shape, shards, smallest, high):
    def one(axis_at, parts):
        steps = jax.random.uniform(jax.random.fold_in(jax.random.fold_in(key, 6), axis_at), (parts,), jnp.float32, smallest / len(shards), high / len(shards))
        return jnp.repeat(jnp.exp(steps), shape[axis_at] // parts).reshape((-1,) + (1,) * (len(shape) - axis_at - 1))

    gain = one(*shards[0])
    for cut in shards[1:]:
        gain = gain * one(*cut)
    return gain


def scatter_about(key, extent, width, limit, split=(), kind=jnp.bfloat16):
    entries = width * jax.random.normal(key, extent, jnp.float32)
    if split:
        entries = entries * steps_of(key, extent, split, -0.22, 0.18)
    return jnp.clip(entries, -limit, limit).astype(kind)


def setup_inputs(seed: int = 0) -> dict:
    streams_of = jax.random.split(jax.random.key(seed), 7)
    state = scatter_about(streams_of[0], (C, NX, NY, NZ), 1.0, 6.0, ((1, 64), (2, 4)))
    target = scatter_about(streams_of[1], (C, NX, NY, NZ), 1.0, 6.0, ((1, 64), (2, 4)))
    spectral_weight = scatter_about(streams_of[2], (2, C, MX, MYZ, C), (2 * C) ** -0.5, 0.375, ((3, 256),))
    direction_weight = scatter_about(streams_of[3], (2, C, MX, MYZ, C), (2 * C) ** -0.5, 0.375, ((3, 256),))
    inner_weight = scatter_about(streams_of[4], (C, FF), C ** -0.5, 0.5)
    outer_weight = scatter_about(streams_of[5], (FF, C), FF ** -0.5, 0.25)
    return dict(state=state, target=target, spectral_weight=spectral_weight, direction_weight=direction_weight, inner_weight=inner_weight, outer_weight=outer_weight)


HIGHEST_PRECISION = lax.Precision.HIGHEST

def signed_frequency(number):
    ladder = jnp.arange(number, dtype=jnp.int32)
    return jnp.where(ladder < number // 2, ladder, ladder - number)

def phase_table(positions, frequencies, length):
    wrapped = positions[:, None] * frequencies[None, :] % length
    angles = wrapped.astype(jnp.float32) * (2.0 * math.pi / length)
    return (jnp.cos(angles), jnp.sin(angles))

def plane_forward(positions, length):
    cosine, sine = phase_table(positions, signed_frequency(MX), length)
    return jnp.stack([jnp.stack([cosine, -sine]), jnp.stack([sine, cosine])])

def plane_inverse(positions, length):
    cosine, sine = phase_table(positions, signed_frequency(MX), length)
    return jnp.stack([jnp.stack([cosine.T, sine.T]), jnp.stack([-sine.T, cosine.T])])

def forward_rows(cells, row_start, factor):
    row_count = cells.shape[3]
    row_pos = row_start + jnp.arange(row_count, dtype=jnp.int32)
    cos_z, sin_z = phase_table(jnp.arange(NZ, dtype=jnp.int32), jnp.arange(MZ, dtype=jnp.int32), NZ)
    cos_y, sin_y = phase_table(row_pos, signed_frequency(MY), NY)
    table_z = jnp.concatenate([cos_z, -sin_z], axis=1)
    table_y = jnp.concatenate([cos_y, -sin_y], axis=1)
    along_z = jnp.einsum('scxyz,zm->scxym', cells, table_z, precision=HIGHEST_PRECISION)
    products = jnp.einsum('scxym,yk->scxkm', along_z, table_y, precision=HIGHEST_PRECISION)
    real_part = products[:, :, :, :MY, :MZ] - products[:, :, :, MY:, MZ:]
    imag_part = products[:, :, :, :MY, MZ:] + products[:, :, :, MY:, :MZ]
    stacked = jnp.stack([real_part, imag_part], axis=1) * factor
    return stacked.reshape(stacked.shape[:4] + (MY * MZ,))

def inverse_rows(modes, row_start, row_count, factor):
    row_pos = row_start + jnp.arange(row_count, dtype=jnp.int32)
    cos_y, sin_y = phase_table(row_pos, signed_frequency(MY), NY)
    table_y = jnp.stack([jnp.stack([cos_y.T, sin_y.T]), jnp.stack([-sin_y.T, cos_y.T])])
    cos_z, sin_z = phase_table(jnp.arange(NZ, dtype=jnp.int32), jnp.arange(MZ, dtype=jnp.int32), NZ)
    table_z = jnp.stack([cos_z.T, -sin_z.T])
    halfway = jnp.einsum('spcxkm,pqky->sqcxym', modes, table_y, precision=HIGHEST_PRECISION)
    return jnp.einsum('sqcxym,qmz->scxyz', halfway, table_z, precision=HIGHEST_PRECISION) * factor

def round_half(values):
    return lax.optimization_barrier(values.astype(jnp.bfloat16)).astype(jnp.float32)

def reference(state, target, spectral_weight, direction_weight, inner_weight, outer_weight):
    points = NX * NY * NZ
    kept_modes = MX * MY * MZ
    forward_factor = 1.0 / math.sqrt(points)
    inverse_factor = 2.0 / math.sqrt(kept_modes)
    loss_scale = 0.5 * math.sqrt(kept_modes / points)
    inner_float = inner_weight.astype(jnp.float32)
    outer_float = outer_weight.astype(jnp.float32)
    state_planes = jnp.moveaxis(state, 1, 0)
    target_planes = jnp.moveaxis(target, 1, 0)

    def plane_modes(state_plane):
        cells = state_plane.astype(jnp.float32)[None, :, None]
        return forward_rows(cells, 0, forward_factor)[0, :, :, 0]
    yz_modes = lax.map(plane_modes, state_planes)
    x_forward = plane_forward(jnp.arange(NX, dtype=jnp.int32), NX)
    spectra = jnp.einsum('xpcj,pqxk->qckj', yz_modes, x_forward, precision=HIGHEST_PRECISION)

    def mix_one(operands):
        weight_one, direction_one, spectra_one = operands
        weights = jnp.stack([weight_one, direction_one]).astype(jnp.float32)
        products = jnp.einsum('spcjo,qcj->spqoj', weights, spectra_one, precision=HIGHEST_PRECISION)
        real_part = products[:, 0, 0] - products[:, 1, 1]
        imag_part = products[:, 0, 1] + products[:, 1, 0]
        return jnp.stack([real_part, imag_part], axis=1)
    mode_sums = lax.map(mix_one, (jnp.moveaxis(spectral_weight, 2, 0), jnp.moveaxis(direction_weight, 2, 0), jnp.moveaxis(spectra, 2, 0)))
    x_inverse = plane_inverse(jnp.arange(NX, dtype=jnp.int32), NX)
    field_modes = jnp.einsum('kspoj,pqkx->xsqoj', mode_sums, x_inverse, precision=HIGHEST_PRECISION)

    def plane_step(operands):
        state_plane, target_plane, modes_plane = operands
        fields = inverse_rows(modes_plane.reshape(2, 2, C, 1, MY, MZ), 0, NY, inverse_factor)[:, :, 0]
        primal_field = round_half(fields[0])
        tangent_field = round_half(fields[1])
        layer_input = state_plane.astype(jnp.float32) + primal_field
        input_half = round_half(layer_input)
        hidden = jnp.einsum('cyz,cf->yzf', input_half, inner_float)
        gauss_mass = 0.5 * (1.0 + lax.erf(hidden * math.sqrt(0.5)))
        gauss_density = jnp.exp(-0.5 * hidden * hidden) / math.sqrt(2.0 * math.pi)
        slope_term = gauss_mass + hidden * gauss_density
        bend_term = gauss_density * (2.0 - hidden * hidden)
        activation = round_half(hidden * gauss_mass)
        output = layer_input + jnp.einsum('yzf,fc->cyz', activation, outer_float)
        seed_primal = loss_scale * (output - target_plane.astype(jnp.float32))
        hidden_tangent = jnp.einsum('cyz,cf->yzf', tangent_field, inner_float)
        activation_tangent = round_half(slope_term * hidden_tangent)
        seed_tangent = loss_scale * (tangent_field + jnp.einsum('yzf,fc->cyz', activation_tangent, outer_float))
        back_primal = jnp.einsum('cyz,fc->yzf', round_half(seed_primal), outer_float)
        back_tangent = jnp.einsum('cyz,fc->yzf', round_half(seed_tangent), outer_float)
        delta_primal = round_half(slope_term * back_primal)
        delta_tangent = round_half(bend_term * hidden_tangent * back_primal + slope_term * back_tangent)
        cotangent_primal = seed_primal + jnp.einsum('yzf,cf->cyz', delta_primal, inner_float)
        cotangent_tangent = seed_tangent + jnp.einsum('yzf,cf->cyz', delta_tangent, inner_float)
        cotangent_pair = jnp.stack([cotangent_primal, cotangent_tangent])[:, :, None]
        return forward_rows(cotangent_pair, 0, inverse_factor)[:, :, :, 0]
    cotangent_yz = lax.map(plane_step, (state_planes, target_planes, field_modes))
    adjoint_modes = jnp.einsum('xspcj,pqxk->ksqcj', cotangent_yz, x_forward, precision=HIGHEST_PRECISION)

    def outer_one(operands):
        spectra_one, adjoint_one = operands
        products = jnp.einsum('pcj,sqoj->spqcjo', spectra_one, adjoint_one, precision=HIGHEST_PRECISION)
        first_part = products[:, 0, 0] + products[:, 1, 1]
        second_part = products[:, 0, 1] - products[:, 1, 0]
        return jnp.stack([first_part, second_part], axis=1).astype(jnp.bfloat16)
    result_pair = lax.map(outer_one, (jnp.moveaxis(spectra, 2, 0), adjoint_modes))
    result_pair = jnp.moveaxis(result_pair, 0, 3)
    return (result_pair[0], result_pair[1])
```

```python
import math

import jax
import jax.numpy as jnp
import numpy as np
from jax import lax
from jax.sharding import Mesh
from jax.sharding import PartitionSpec as P

C = 128
NX = 64
NY = 128
NZ = 128
MX = 16
MY = 32
MZ = 16
ROWS = 32

GX = ("xl", "y", "z")
COL = ("xh", "co")
WIDE = GX + ("xh",)

HIGHEST = lax.Precision.HIGHEST


def signed(number):
    ladder = np.arange(number)
    return np.where(ladder < number // 2, ladder, ladder - number)


def angles(positions, frequencies, length):
    return (np.outer(positions, frequencies) % length) * (2.0 * math.pi / length)


def z_forward():
    a = angles(np.arange(NZ), np.arange(MZ), NZ)
    return np.stack([np.cos(a), -np.sin(a)], axis=1).astype(np.float32)


def y_forward_all():
    a = angles(np.arange(NY), signed(MY), NY)
    c, s = np.cos(a), np.sin(a)
    t = np.stack([np.stack([c, -s], -1), np.stack([s, c], -1)])
    return t.reshape(2, NY // ROWS, ROWS, MY, 2).astype(np.float32)


def x_forward():
    a = angles(np.arange(NX), signed(MX), NX)
    c, s = np.cos(a), np.sin(a)
    return np.stack([np.stack([c, -s], -1), np.stack([s, c], -1)]).astype(np.float32)


def x_inverse():
    a = angles(np.arange(NX), signed(MX), NX)
    c, s = np.cos(a), np.sin(a)
    return np.stack([np.stack([c, s], -1), np.stack([-s, c], -1)]).astype(np.float32)


def y_inverse_all():
    a = angles(np.arange(NY), signed(MY), NY)
    c, s = np.cos(a), np.sin(a)
    t = np.stack([np.stack([c, s], -1), np.stack([-s, c], -1)])
    return t.reshape(2, NY // ROWS, ROWS, MY, 2).astype(np.float32)


def z_inverse():
    a = angles(np.arange(NZ), np.arange(MZ), NZ)
    return np.stack([np.cos(a), -np.sin(a)], axis=1).astype(np.float32)


def to_owners(modes, fields):
    core = lax.axis_index("co")
    split = modes.reshape(MY, 2, 2, 2, 2, fields, 2, C)
    keep = lax.dynamic_index_in_dim(split, core, 3, keepdims=False)
    give = lax.dynamic_index_in_dim(split, 1 - core, 3, keepdims=False)
    summed = keep + lax.ppermute(give, "co", [(0, 1), (1, 0)])
    return lax.all_to_all(summed.reshape(2 * NX, 2 * fields * 2, C), WIDE, 0, 0, tiled=True)


def forward_modes(cells, y_table):
    fields = cells.shape[0]
    along_z = jnp.einsum("syzc,zpk->sypkc", cells, z_forward(), precision=HIGHEST)
    modes = jnp.einsum("sypkc,pyjq->jksqc", along_z, y_table, precision=HIGHEST)
    return to_owners(modes, fields)


def at_owner(received, fields, factor):
    rows = received.reshape(NX, 2, 2, fields, 2, C)
    return jnp.einsum("xhmspc,pxkq->sqkmc", rows, x_forward() * np.float32(factor), precision=HIGHEST)


def local(state, target, spectral_weight, direction_weight, inner_weight, outer_weight):
    points = NX * NY * NZ
    kept_modes = MX * MY * MZ
    forward_factor = 1.0 / math.sqrt(points)
    inverse_factor = 2.0 / math.sqrt(kept_modes)
    loss_scale = 0.5 * math.sqrt(kept_modes / points)
    column = lax.axis_index(COL)
    y_fwd = lax.dynamic_index_in_dim(jnp.asarray(y_forward_all()), column, 1, keepdims=False)
    y_inv = lax.dynamic_index_in_dim(jnp.asarray(y_inverse_all()), column, 1, keepdims=False)

    state_rows = state[:, 0].transpose(1, 2, 0)
    target_rows = target[:, 0].transpose(1, 2, 0)
    state_float = state_rows.astype(jnp.float32)
    spectra = at_owner(forward_modes(state_float[None], y_fwd), 1, forward_factor)[0]

    weights = jnp.stack([spectral_weight, direction_weight]).astype(jnp.float32)
    products = jnp.einsum("spckmo,qkmc->spqkmo", weights, spectra, precision=HIGHEST)
    sums = jnp.stack([products[:, 0, 0] - products[:, 1, 1], products[:, 0, 1] + products[:, 1, 0]], 1)
    planes = jnp.einsum("spkmo,pxkq->xmsqo", sums, x_inverse() * np.float32(inverse_factor), precision=HIGHEST)
    both = jnp.broadcast_to(planes[:, None], (NX, 2, 2, 2, 2, C)).reshape(2 * NX, 8, C)
    arrived = lax.all_to_all(both, WIDE, 0, 0, tiled=True)
    other = lax.ppermute(arrived, "co", [(0, 1), (1, 0)])
    core = lax.axis_index("co")
    low = jnp.where(core == 0, arrived, other)
    high = jnp.where(core == 0, other, arrived)
    whole = jnp.stack([low, high], 1).reshape(MY, 2, 2, 2, 2, 2, 2, C)
    whole = whole.reshape(MY, MZ, 2, 2, C)
    halfway = jnp.einsum("jkspc,pyjq->sykqc", whole, y_inv, precision=HIGHEST)
    fields = jnp.einsum("sykqc,zqk->syzc", halfway, z_inverse(), precision=HIGHEST)

    primal_field = fields[0].astype(jnp.bfloat16)
    tangent_field = fields[1].astype(jnp.bfloat16)
    layer_input = state_float + primal_field.astype(jnp.float32)
    f32 = jnp.float32

    def mix(eq, a, b):
        return jnp.einsum(eq, a, b, preferred_element_type=f32)

    hidden = mix("yzc,cf->yzf", layer_input.astype(jnp.bfloat16), inner_weight)
    gauss_mass = 0.5 * (1.0 + lax.erf(hidden * math.sqrt(0.5)))
    gauss_density = jnp.exp(-0.5 * hidden * hidden) / math.sqrt(2.0 * math.pi)
    slope_term = gauss_mass + hidden * gauss_density
    activation = (hidden * gauss_mass).astype(jnp.bfloat16)
    output = layer_input + mix("yzf,fc->yzc", activation, outer_weight)
    seed_primal = loss_scale * (output - target_rows.astype(f32))
    hidden_tangent = mix("yzc,cf->yzf", tangent_field, inner_weight)
    activation_tangent = (slope_term * hidden_tangent).astype(jnp.bfloat16)
    seed_tangent = loss_scale * (tangent_field.astype(f32) + mix("yzf,fc->yzc", activation_tangent, outer_weight))
    back_primal = mix("yzc,fc->yzf", seed_primal.astype(jnp.bfloat16), outer_weight)
    back_tangent = mix("yzc,fc->yzf", seed_tangent.astype(jnp.bfloat16), outer_weight)
    delta_primal = (slope_term * back_primal).astype(jnp.bfloat16)
    bend_term = gauss_density * (2.0 - hidden * hidden)
    delta_tangent = (bend_term * hidden_tangent * back_primal + slope_term * back_tangent).astype(jnp.bfloat16)
    cotangent_primal = seed_primal + mix("yzf,cf->yzc", delta_primal, inner_weight)
    cotangent_tangent = seed_tangent + mix("yzf,cf->yzc", delta_tangent, inner_weight)

    pair = jnp.stack([cotangent_primal, cotangent_tangent])
    adjoint = at_owner(forward_modes(pair, y_fwd), 2, inverse_factor)

    spectra_c = spectra.transpose(0, 3, 1, 2)[:, :, :, :, None]
    real, imag = spectra_c[0], spectra_c[1]

    def outer(one):
        re, im = one[0][None], one[1][None]
        return jnp.stack([real * re + imag * im, real * im - imag * re]).astype(jnp.bfloat16)

    return outer(adjoint[0]), outer(adjoint[1])


def solution(mesh):
    fine = Mesh(mesh.devices.reshape(2, 4, 8, 2, 2), GX + COL)
    grid = P(None, GX, COL, None)
    blocks = P(None, None, None, GX + COL, None)
    return jax.shard_map(
        local,
        mesh=fine,
        in_specs=(grid, grid, blocks, blocks, P(), P()),
        out_specs=(blocks, blocks),
        check_vma=False,
    )
```

```python
import math

import jax
import jax.numpy as jnp
import ml_dtypes
import numpy as np
from jax import lax
from jax.experimental import pallas as pl
from jax.experimental.pallas import tpu as pltpu
from jax.sharding import Mesh
from jax.sharding import PartitionSpec as P

C = 128
FF = 512
NX = 64
NY = 128
NZ = 128
MX = 16
MY = 32
MZ = 16
ROWS = 32
COLUMNS = 4
POINTS = NX * NY * NZ
KEPT = MX * MY * MZ
FORWARD_FACTOR = 1.0 / math.sqrt(POINTS)
INVERSE_FACTOR = 2.0 / math.sqrt(KEPT)
LOSS_SCALE = 0.5 * math.sqrt(KEPT / POINTS)
ROWS_A_STEP = 4
CHUNK = ROWS_A_STEP * NZ
CB = 16

GX = ("xl", "y", "z")
COL = ("xh", "co")
WIDE = GX + ("xh",)
F32 = jnp.float32
BF16 = jnp.bfloat16


def params():
    return pltpu.CompilerParams(dimension_semantics=("arbitrary",), vmem_limit_bytes=44 * 1024 * 1024)


def signed(number):
    ladder = np.arange(number)
    return np.where(ladder < number // 2, ladder, ladder - number)


def angles(positions, frequencies, length):
    return (np.outer(positions, frequencies) % length) * (2.0 * math.pi / length)


def halves(table):
    high = table.astype(ml_dtypes.bfloat16)
    low = (table - high.astype(np.float64)).astype(ml_dtypes.bfloat16)
    return high, low


def wide(table):
    high, low = halves(table)
    return np.concatenate([high, high, low], axis=-1)


def tall(table):
    high, low = halves(table)
    return np.concatenate([high, low], axis=-2)


def rotation(positions, frequencies, length, sign):
    a = angles(positions, frequencies, length)
    c, s = np.cos(a), sign * np.sin(a)
    return np.stack([np.stack([c, -s]), np.stack([s, c])])


def z_order(core):
    order = []
    for which in range(2):
        co = core if which == 0 else 1 - core
        for zh in range(2):
            for xh in range(2):
                for m in range(2):
                    order.append(8 * zh + 4 * xh + 2 * co + m)
    return np.array(order)


def z_tables():
    inverse, forward = [], []
    for core in range(2):
        a = angles(np.arange(NZ), z_order(core), NZ)
        inverse.append(wide(np.stack([np.cos(a), -np.sin(a)], -1).reshape(NZ, 2 * MZ)))
        forward.append(tall(np.stack([np.cos(a), -np.sin(a)], -1).reshape(NZ, 2 * MZ).T))
    return np.stack(inverse), np.stack(forward)


def y_tables():
    inverse, forward = [], []
    for column in range(COLUMNS):
        rows = column * ROWS + np.arange(ROWS)
        r = rotation(rows, signed(MY), NY, 1.0)
        inverse.append(wide(r.transpose(0, 2, 1, 3).reshape(2 * ROWS, 2 * MY)))
        r = rotation(rows, signed(MY), NY, -1.0)
        forward.append(wide(r.transpose(0, 3, 1, 2).reshape(2 * MY, 2 * ROWS)))
    return np.stack(inverse), np.stack(forward)


def x_forward_table(fields, factor):
    r = rotation(np.arange(NX), signed(MX), NX, -1.0) * factor
    t = np.zeros((fields, 2, MX, 2, NX, 2, 2, fields, 2))
    for s in range(fields):
        for m in range(2):
            for xh in range(2):
                t[s, :, :, m, :, xh, m, s, :] = r.transpose(0, 3, 2, 1)
    return tall(t.reshape(fields * 2 * MX * 2, NX * 2 * 2 * fields * 2))


def x_inverse_table(factor):
    r = rotation(np.arange(NX), signed(MX), NX, 1.0) * factor
    t = np.zeros((NX, 2, 2, 2, 2, 2, MX, 2))
    for s in range(2):
        for m in range(2):
            t[:, m, s, :, s, :, :, m] = r.transpose(2, 0, 1, 3)
    return wide(t.reshape(NX * 8, 128))


def dot(a, b):
    return jnp.dot(a, b, preferred_element_type=F32)


def two(values):
    high = values.astype(BF16)
    return high, (values - high.astype(F32)).astype(BF16)


def three(values):
    high, low = two(values)
    return jnp.concatenate([high, low, high], axis=0)


def tall_dot(table, values):
    rows = table.shape[0] // 2
    high, low = two(values)
    first = dot(table, high)
    return first[:rows] + first[rows:] + dot(table[:rows], low)


def field_kernel(
    mine, other, state, target, w1, w2, w1t, w2t, yi, zi, zf, yf, keep, give, half, after
):
    step = pl.program_id(0)

    @pl.when(step == 0)
    def _():
        for k in range(MZ):
            source = mine if k < 8 else other
            base = (k % 8) // 2 * 8 + k % 2 * 4
            parts = []
            for s in range(2):
                p = [source[pl.ds(base + 2 * s + i, MY, stride=32), :] for i in range(2)]
                parts.append(jnp.concatenate(p, axis=0))
            rows = dot(yi[...], three(jnp.concatenate(parts, axis=1)))
            for s in range(2):
                half[s, pl.ds(k * 64, 64), :] = rows[:, s * C : (s + 1) * C]

    fields = []
    for i in range(ROWS_A_STEP):
        y = step * ROWS_A_STEP + i
        taken = [half[s, pl.ds(y, 2 * MZ, stride=ROWS), :] for s in range(2)]
        fields.append(dot(zi[...], three(jnp.concatenate(taken, axis=1))))
    fields = jnp.concatenate(fields, axis=0).astype(BF16)
    primal, tangent = fields[:, :C], fields[:, C:]
    layer_input = state[...].astype(F32) + primal.astype(F32)
    hidden = dot(layer_input.astype(BF16), w1[...])
    mass = 0.5 * (1.0 + lax.erf(hidden * math.sqrt(0.5)))
    density = jnp.exp(-0.5 * hidden * hidden) * (1.0 / math.sqrt(2.0 * math.pi))
    slope = mass + hidden * density
    activation = (hidden * mass).astype(BF16)
    seed_primal = LOSS_SCALE * (layer_input + dot(activation, w2[...]) - target[...].astype(F32))
    hidden_tangent = dot(tangent, w1[...])
    activation_tangent = (slope * hidden_tangent).astype(BF16)
    seed_tangent = LOSS_SCALE * (tangent.astype(F32) + dot(activation_tangent, w2[...]))
    back_primal = dot(seed_primal.astype(BF16), w2t[...])
    back_tangent = dot(seed_tangent.astype(BF16), w2t[...])
    delta_primal = (slope * back_primal).astype(BF16)
    bend = density * (2.0 - hidden * hidden)
    delta_tangent = (bend * hidden_tangent * back_primal + slope * back_tangent).astype(BF16)
    cotangents = jnp.concatenate(
        [seed_primal + dot(delta_primal, w1t[...]), seed_tangent + dot(delta_tangent, w1t[...])], axis=1
    )
    for i in range(ROWS_A_STEP):
        rows = tall_dot(zf[...], cotangents[i * NZ : (i + 1) * NZ])
        start = pl.multiple_of((step * ROWS_A_STEP + i) * 2 * MZ, 2 * MZ)
        for s in range(2):
            after[s, pl.ds(start, 2 * MZ), :] = rows[:, s * C : (s + 1) * C]

    @pl.when(step == ROWS // ROWS_A_STEP - 1)
    def _():
        for k in range(MZ):
            sink = keep if k < 8 else give
            base = (k % 8) // 2 * 8 + k % 2 * 4
            parts = []
            for s in range(2):
                q = [after[s, pl.ds(2 * k + i, ROWS, stride=2 * MZ), :] for i in range(2)]
                parts.append(jnp.concatenate(q, axis=0))
            rows = dot(yf[...], three(jnp.concatenate(parts, axis=1)))
            for s in range(2):
                for r in range(2):
                    sink[pl.ds(base + 2 * s + r, MY, stride=32), :] = rows[
                        r * MY : (r + 1) * MY, s * C : (s + 1) * C
                    ]


def whole(shape):
    return pl.BlockSpec(shape, lambda i: (0,) * len(shape))


def field_stage(mine, other, state, target, w1, w2, yi, zi, zf, yf):
    operands = (mine, other, state, target, w1, w2, w1.T, w2.T, yi, zi, zf, yf)
    moving = pl.BlockSpec((CHUNK, C), lambda i: (i, 0))
    specs = [moving if i in (2, 3) else whole(a.shape) for i, a in enumerate(operands)]
    shape = jax.ShapeDtypeStruct((1024, C), F32)
    return pl.pallas_call(
        field_kernel,
        grid=(ROWS // ROWS_A_STEP,),
        in_specs=specs,
        out_specs=(whole((1024, C)), whole((1024, C))),
        out_shape=(shape, shape),
        scratch_shapes=[pltpu.VMEM((2, 1024, C), F32), pltpu.VMEM((2, 1024, C), F32)],
        compiler_params=params(),
    )(*operands)


def mix_kernel(received, weight, direction, xf, xi, spectra, planes, total):
    step = pl.program_id(0)

    @pl.when(step == 0)
    def _():
        spectra[...] = tall_dot(xf[...], received[...])
        total[...] = jnp.zeros_like(total)

    turned = pltpu.roll(spectra[...], C - step * CB, 1)
    sums = [total[i] for i in range(4)]
    for j in range(CB):
        column = jnp.broadcast_to(turned[:, j : j + 1], (64, C))
        real, imag = column[:32], column[32:]
        for s, w in ((0, weight), (1, direction)):
            wr, wi = w[0, j].astype(F32), w[1, j].astype(F32)
            sums[2 * s] = sums[2 * s] + (wr * real - wi * imag)
            sums[2 * s + 1] = sums[2 * s + 1] + (wr * imag + wi * real)
    for i in range(4):
        total[i] = sums[i]

    @pl.when(step == C // CB - 1)
    def _():
        out = dot(xi[...], three(jnp.concatenate(sums, axis=0))).reshape(NX, 8, C)
        planes[:, 0] = out
        planes[:, 1] = out


def mix_stage(received, weight, direction):
    xf = x_forward_table(1, FORWARD_FACTOR)
    xi = x_inverse_table(INVERSE_FACTOR)
    weight = weight.reshape(2, C, 32, C)
    direction = direction.reshape(2, C, 32, C)
    moving = pl.BlockSpec((2, CB, 32, C), lambda i: (0, i, 0, 0))
    return pl.pallas_call(
        mix_kernel,
        grid=(C // CB,),
        in_specs=[whole(received.shape), moving, moving, whole(xf.shape), whole(xi.shape)],
        out_specs=(whole((64, C)), whole((NX, 2, 8, C))),
        out_shape=(jax.ShapeDtypeStruct((64, C), F32), jax.ShapeDtypeStruct((NX, 2, 8, C), F32)),
        scratch_shapes=[pltpu.VMEM((4, 32, C), F32)],
        compiler_params=params(),
    )(received, weight, direction, jnp.asarray(xf), jnp.asarray(xi))


def outer_kernel(received, spectra, xf, gradient, curvature, adjoint):
    step = pl.program_id(0)

    @pl.when(step == 0)
    def _():
        adjoint[...] = tall_dot(xf[...], received[...])

    turned = pltpu.roll(spectra[...], C - step * CB, 1)
    pieces = [adjoint[32 * i : 32 * i + 32, :] for i in range(4)]
    for j in range(CB):
        column = jnp.broadcast_to(turned[:, j : j + 1], (64, C))
        real, imag = column[:32], column[32:]
        for s, sink in ((0, gradient), (1, curvature)):
            re, im = pieces[2 * s], pieces[2 * s + 1]
            sink[0, j] = (real * re + imag * im).astype(BF16)
            sink[1, j] = (real * im - imag * re).astype(BF16)


def outer_stage(received, spectra):
    xf = x_forward_table(2, INVERSE_FACTOR)
    moving = pl.BlockSpec((2, CB, 32, C), lambda i: (0, i, 0, 0))
    shape = jax.ShapeDtypeStruct((2, C, 32, C), BF16)
    return pl.pallas_call(
        outer_kernel,
        grid=(C // CB,),
        in_specs=[whole(received.shape), whole(spectra.shape), whole(xf.shape)],
        out_specs=(moving, moving),
        out_shape=(shape, shape),
        scratch_shapes=[pltpu.VMEM((128, C), F32)],
        compiler_params=params(),
    )(received, spectra, jnp.asarray(xf))


def to_owners(keep, give):
    summed = keep + lax.ppermute(give, "co", [(0, 1), (1, 0)])
    return lax.all_to_all(summed.reshape(2 * NX, -1, C), WIDE, 0, 0, tiled=True)


def state_modes(cells, core, column):
    a = angles(np.arange(NZ), np.arange(MZ), NZ)
    z_table = np.stack([np.cos(a), -np.sin(a)], axis=1).astype(np.float32)
    rows = np.arange(NY)
    r = rotation(rows, signed(MY), NY, -1.0).transpose(1, 2, 3, 0)
    y_table = r.reshape(2, COLUMNS, ROWS, MY, 2).astype(np.float32)
    y_table = lax.dynamic_index_in_dim(jnp.asarray(y_table), column, 1, keepdims=False)
    along_z = jnp.einsum("yzc,zpk->ypkc", cells, z_table, precision=lax.Precision.HIGHEST)
    modes = jnp.einsum("ypkc,pyjq->jkqc", along_z, y_table, precision=lax.Precision.HIGHEST)
    split = modes.reshape(MY, 2, 2, 2, 2, 2, C)
    keep = lax.dynamic_index_in_dim(split, core, 3, keepdims=False)
    give = lax.dynamic_index_in_dim(split, 1 - core, 3, keepdims=False)
    return keep, give


def local(state, target, spectral_weight, direction_weight, inner_weight, outer_weight):
    column = lax.axis_index(COL)
    core = lax.axis_index("co")

    def pick(table, index):
        return lax.dynamic_index_in_dim(jnp.asarray(table), index, 0, keepdims=False)

    yi, yf = (pick(t, column) for t in y_tables())
    zi, zf = (pick(t, core) for t in z_tables())
    state_rows = state[:, 0].transpose(1, 2, 0)
    target_rows = target[:, 0].transpose(1, 2, 0).reshape(ROWS * NZ, C)
    received = to_owners(*state_modes(state_rows.astype(F32), core, column))
    spectra, planes = mix_stage(received.reshape(512, C), spectral_weight, direction_weight)
    arrived = lax.all_to_all(planes.reshape(2 * NX, 8, C), WIDE, 0, 0, tiled=True).reshape(1024, C)
    other = lax.ppermute(arrived, "co", [(0, 1), (1, 0)])
    keep, give = field_stage(
        arrived, other, state_rows.reshape(ROWS * NZ, C), target_rows, inner_weight, outer_weight, yi, zi, zf, yf
    )
    adjoint = to_owners(keep, give)
    gradient, curvature = outer_stage(adjoint.reshape(1024, C), spectra)
    shape = (2, C, MX, 2, C)
    return gradient.reshape(shape), curvature.reshape(shape)


def solution(mesh):
    fine = Mesh(mesh.devices.reshape(2, 4, 8, 2, 2), GX + COL)
    grid = P(None, GX, COL, None)
    blocks = P(None, None, None, GX + COL, None)
    return jax.shard_map(
        local,
        mesh=fine,
        in_specs=(grid, grid, blocks, blocks, P(), P()),
        out_specs=(blocks, blocks),
        check_vma=False,
    )
```

```python
import math

import jax
import jax.numpy as jnp
import ml_dtypes
import numpy as np
from jax import lax
from jax.experimental import pallas as pl
from jax.experimental.pallas import tpu as pltpu
from jax.sharding import Mesh
from jax.sharding import PartitionSpec as P

C = 128
FF = 512
NX = 64
NY = 128
NZ = 128
MX = 16
MY = 32
MZ = 16
ROWS = 32
COLUMNS = 4
POINTS = NX * NY * NZ
KEPT = MX * MY * MZ
FORWARD_FACTOR = 1.0 / math.sqrt(POINTS)
INVERSE_FACTOR = 2.0 / math.sqrt(KEPT)
LOSS_SCALE = 0.5 * math.sqrt(KEPT / POINTS)
ROWS_A_STEP = 16
CHUNK = ROWS_A_STEP * NZ
CB = 64

GX = ("xl", "y", "z")
COL = ("xh", "co")
WIDE = ("y", "z", "xl", "xh")
F32 = jnp.float32
BF16 = jnp.bfloat16


def params():
    return pltpu.CompilerParams(dimension_semantics=("arbitrary",), vmem_limit_bytes=44 * 1024 * 1024)


def signed(number):
    ladder = np.arange(number)
    return np.where(ladder < number // 2, ladder, ladder - number)


def angles(positions, frequencies, length):
    return (np.outer(positions, frequencies) % length) * (2.0 * math.pi / length)


def halves(table):
    high = table.astype(ml_dtypes.bfloat16)
    low = (table - high.astype(np.float64)).astype(ml_dtypes.bfloat16)
    return high, low


def wide(table):
    high, low = halves(table)
    return np.concatenate([high, high, low], axis=-1)


def tall(table):
    high, low = halves(table)
    return np.concatenate([high, low], axis=-2)


def rotation(positions, frequencies, length, sign):
    a = angles(positions, frequencies, length)
    c, s = np.cos(a), sign * np.sin(a)
    return np.stack([np.stack([c, -s]), np.stack([s, c])])


def z_order(core):
    order = []
    for which in range(2):
        co = core if which == 0 else 1 - core
        for zh in range(2):
            for xh in range(2):
                for m in range(2):
                    order.append(8 * zh + 4 * xh + 2 * co + m)
    return np.array(order)


def z_tables():
    inverse, forward = [], []
    for core in range(2):
        a = angles(np.arange(NZ), z_order(core), NZ)
        inverse.append(wide(np.stack([np.cos(a), -np.sin(a)], -1).reshape(NZ, 2 * MZ)))
        forward.append(tall(np.stack([np.cos(a), -np.sin(a)], -1).reshape(NZ, 2 * MZ).T))
    return np.stack(inverse), np.stack(forward)


def y_tables():
    inverse, forward = [], []
    for column in range(COLUMNS):
        rows = column * ROWS + np.arange(ROWS)
        r = rotation(rows, signed(MY), NY, 1.0)
        inverse.append(wide(r.transpose(0, 2, 1, 3).reshape(2 * ROWS, 2 * MY)))
        r = rotation(rows, signed(MY), NY, -1.0)
        forward.append(wide(r.transpose(0, 3, 1, 2).reshape(2 * MY, 2 * ROWS)))
    return np.stack(inverse), np.stack(forward)


def x_places():
    return np.arange(NX).reshape(2, 4, 8).transpose(1, 2, 0).reshape(NX)


def x_forward_table(fields, factor):
    r = rotation(x_places(), signed(MX), NX, -1.0) * factor
    t = np.zeros((fields, 2, MX, 2, NX, 2, 2, fields, 2))
    for s in range(fields):
        for m in range(2):
            for xh in range(2):
                t[s, :, :, m, :, xh, m, s, :] = r.transpose(0, 3, 2, 1)
    return tall(t.reshape(fields * 2 * MX * 2, NX * 2 * 2 * fields * 2))


def x_inverse_table(factor):
    r = rotation(x_places(), signed(MX), NX, 1.0) * factor
    t = np.zeros((NX, 2, 2, 2, 2, 2, MX, 2))
    for s in range(2):
        for m in range(2):
            t[:, m, s, :, s, :, :, m] = r.transpose(2, 0, 1, 3)
    return wide(t.reshape(NX * 8, 128))


def dot(a, b):
    return jnp.dot(a, b, preferred_element_type=F32)


def two(values):
    high = values.astype(BF16)
    return high, (values - high.astype(F32)).astype(BF16)


def three(values):
    high, low = two(values)
    return jnp.concatenate([high, low, high], axis=0)


def tall_dot(table, values):
    rows = table.shape[0] // 2
    high, low = two(values)
    first = dot(table, high)
    return first[:rows] + first[rows:] + dot(table[:rows], low)


def mode_rows(k, extra):
    zh, xh, m = k % 8 // 4, k % 4 // 2, k % 2
    return [pl.ds(zh * 32 + xl * 16 + xh * 8 + m * 4 + extra, 16, stride=64) for xl in range(2)]


def state_rows_of(k, extra):
    zh, xh, m = k % 8 // 4, k % 4 // 2, k % 2
    return [pl.ds(zh * 16 + xl * 8 + xh * 4 + m * 2 + extra, 16, stride=32) for xl in range(2)]


def rows_forward(values, fields, table, after, y):
    rows = tall_dot(table, values)
    start = pl.multiple_of(y * 2 * MZ, 2 * MZ)
    for s in range(fields):
        after[s, pl.ds(start, 2 * MZ), :] = rows[:, s * C : (s + 1) * C]


def columns_forward(fields, table, after, keep, give):
    pieces = [(k, s) for k in range(MZ) for s in range(fields)]
    for pair in zip(pieces[::2], pieces[1::2]):
        parts = []
        for k, s in pair:
            q = [after[s, pl.ds(2 * k + i, ROWS, stride=2 * MZ), :] for i in range(2)]
            parts.append(jnp.concatenate(q, axis=0))
        rows = dot(table, three(jnp.concatenate(parts, axis=1)))
        for i, (k, s) in enumerate(pair):
            sink = keep if k < 8 else give
            for r in range(2):
                places = mode_rows(k, 2 * s + r) if fields == 2 else state_rows_of(k, r)
                for xl, place in enumerate(places):
                    at = r * MY + xl * 16
                    sink[place, :] = rows[at : at + 16, i * C : (i + 1) * C]


def state_kernel(place, state, zf, yf, keep, give, after):
    for y in range(0, ROWS, 2):
        pair = jnp.concatenate([state[(y + i) * NZ : (y + i + 1) * NZ] for i in range(2)], axis=1)
        rows = dot(zf[0], pair)
        rows = rows[: 2 * MZ] + rows[2 * MZ :]
        for i in range(2):
            after[0, pl.ds((y + i) * 2 * MZ, 2 * MZ), :] = rows[:, i * C : (i + 1) * C]
    columns_forward(1, yf[0], after, keep, give)


def field_kernel(
    place, mine, other, state, target, w1_, w2_, yi_, zi_, zf_, yf_, keep, give,
    half, after, w1, w2, w1t, w2t, yi, zi, zf, yf, arrivals
):
    step = pl.program_id(0)

    @pl.when(step == 0)
    def _():
        column, core = place[0], place[1]
        pairs = [(yi_.at[column], yi), (zi_.at[core], zi), (w1_, w1), (w2_, w2), (zf_.at[core], zf), (yf_.at[column], yf)]
        copies = [pltpu.make_async_copy(a, b, arrivals.at[i]) for i, (a, b) in enumerate(pairs)]
        for copy in copies:
            copy.start()
        copies[0].wait()
        for k in range(MZ):
            source = mine if k < 8 else other
            parts = []
            for s in range(2):
                p = [source[place, :] for i in range(2) for place in mode_rows(k, 2 * s + i)]
                parts.append(jnp.concatenate(p, axis=0))
            rows = dot(yi[...], three(jnp.concatenate(parts, axis=1)))
            for s in range(2):
                half[s, pl.ds(k * 64, 64), :] = rows[:, s * C : (s + 1) * C]
        for copy in copies[1:]:
            copy.wait()
        w1t[...] = w1[...].T
        w2t[...] = w2[...].T

    first = step * ROWS_A_STEP
    fields = []
    for i in range(ROWS_A_STEP):
        taken = [half[s, pl.ds(first + i, 2 * MZ, stride=ROWS), :] for s in range(2)]
        fields.append(dot(zi[...], three(jnp.concatenate(taken, axis=1))))
    fields = jnp.concatenate(fields, axis=0).astype(BF16)
    primal, tangent = fields[:, :C], fields[:, C:]
    layer_input = state[...].astype(F32) + primal.astype(F32)
    hidden = dot(layer_input.astype(BF16), w1[...])
    mass = 0.5 * (1.0 + lax.erf(hidden * math.sqrt(0.5)))
    density = jnp.exp(-0.5 * hidden * hidden) * (1.0 / math.sqrt(2.0 * math.pi))
    slope = mass + hidden * density
    activation = (hidden * mass).astype(BF16)
    seed_primal = LOSS_SCALE * (layer_input + dot(activation, w2[...]) - target[...].astype(F32))
    hidden_tangent = dot(tangent, w1[...])
    activation_tangent = (slope * hidden_tangent).astype(BF16)
    seed_tangent = LOSS_SCALE * (tangent.astype(F32) + dot(activation_tangent, w2[...]))
    back_primal = dot(seed_primal.astype(BF16), w2t[...])
    back_tangent = dot(seed_tangent.astype(BF16), w2t[...])
    delta_primal = (slope * back_primal).astype(BF16)
    bend = density * (2.0 - hidden * hidden)
    delta_tangent = (bend * hidden_tangent * back_primal + slope * back_tangent).astype(BF16)
    cotangents = [seed_primal + dot(delta_primal, w1t[...]), seed_tangent + dot(delta_tangent, w1t[...])]
    cotangents = jnp.concatenate(cotangents, axis=1)
    for i in range(ROWS_A_STEP):
        rows_forward(cotangents[i * NZ : (i + 1) * NZ], 2, zf[...], after, first + i)

    @pl.when(step == ROWS // ROWS_A_STEP - 1)
    def _():
        columns_forward(2, yf[...], after, keep, give)


def whole(shape):
    return pl.BlockSpec(shape, lambda i: (0,) * len(shape))


def still(shape):
    return pl.BlockSpec(shape, lambda i, place: (0,) * len(shape))


def picked(table, index):
    return pl.BlockSpec((1,) + table.shape[1:], lambda i, place: (place[index], 0, 0))


def call_rows(kernel, place, operands, specs, out_rows, scratch, steps):
    shape = jax.ShapeDtypeStruct((out_rows, C), F32)
    return pl.pallas_call(
        kernel,
        grid_spec=pltpu.PrefetchScalarGridSpec(
            num_scalar_prefetch=1,
            grid=(steps,),
            in_specs=specs,
            out_specs=(still((out_rows, C)), still((out_rows, C))),
            scratch_shapes=scratch,
        ),
        out_shape=(shape, shape),
        compiler_params=params(),
    )(place, *operands)


MOVING = pl.BlockSpec((CHUNK, C), lambda i, place: (i, 0))


def state_stage(place, state, zf, yf):
    specs = [still(state.shape), picked(zf, 1), picked(yf, 0)]
    return call_rows(state_kernel, place, (state, zf, yf), specs, 512, [pltpu.VMEM((1, 1024, C), F32)], 1)


def field_stage(place, mine, other, state, target, weights, tables):
    operands = (mine, other, state, target, *weights, *tables)
    specs = [still(mine.shape), still(other.shape), MOVING, MOVING]
    specs += [pl.BlockSpec(memory_space=pltpu.HBM)] * 6
    scratch = [pltpu.VMEM((2, 1024, C), F32), pltpu.VMEM((2, 1024, C), F32)]
    scratch += [pltpu.VMEM((C, FF), BF16), pltpu.VMEM((FF, C), BF16), pltpu.VMEM((FF, C), BF16), pltpu.VMEM((C, FF), BF16)]
    scratch += [pltpu.VMEM(t.shape[1:], BF16) for t in tables]
    scratch += [pltpu.SemaphoreType.DMA((6,))]
    return call_rows(field_kernel, place, operands, specs, 1024, scratch, ROWS // ROWS_A_STEP)


def mix_kernel(received, weight, direction, xf_, xi_, spectra, planes, total, xf, xi, arrivals):
    step = pl.program_id(0)
    first = pltpu.make_async_copy(xf_, xf, arrivals.at[0])
    second = pltpu.make_async_copy(xi_, xi, arrivals.at[1])

    @pl.when(step == 0)
    def _():
        first.start()
        second.start()
        first.wait()
        spectra[...] = tall_dot(xf[...], received[...])
        total[...] = jnp.zeros_like(total)

    turned = pltpu.roll(spectra[...], C - step * CB, 1)
    sums = [total[i] for i in range(4)]
    for j in range(CB):
        column = jnp.broadcast_to(turned[:, j : j + 1], (64, C))
        real, imag = column[:32], column[32:]
        for s, w in ((0, weight), (1, direction)):
            wr, wi = w[0, j].astype(F32), w[1, j].astype(F32)
            sums[2 * s] = sums[2 * s] + (wr * real - wi * imag)
            sums[2 * s + 1] = sums[2 * s + 1] + (wr * imag + wi * real)
    for i in range(4):
        total[i] = sums[i]

    @pl.when(step == C // CB - 1)
    def _():
        second.wait()
        out = dot(xi[...], three(jnp.concatenate(sums, axis=0))).reshape(NX, 8, C)
        planes[:, 0] = out
        planes[:, 1] = out


def mix_stage(received, weight, direction):
    xf = x_forward_table(1, FORWARD_FACTOR)
    xi = x_inverse_table(INVERSE_FACTOR)
    weight = weight.reshape(2, C, 32, C)
    direction = direction.reshape(2, C, 32, C)
    moving = pl.BlockSpec((2, CB, 32, C), lambda i: (0, i, 0, 0))
    return pl.pallas_call(
        mix_kernel,
        grid=(C // CB,),
        in_specs=[whole(received.shape), moving, moving] + [pl.BlockSpec(memory_space=pltpu.HBM)] * 2,
        out_specs=(whole((64, C)), whole((NX, 2, 8, C))),
        out_shape=(jax.ShapeDtypeStruct((64, C), F32), jax.ShapeDtypeStruct((NX, 2, 8, C), F32)),
        scratch_shapes=[
            pltpu.VMEM((4, 32, C), F32),
            pltpu.VMEM(xf.shape, BF16),
            pltpu.VMEM(xi.shape, BF16),
            pltpu.SemaphoreType.DMA((2,)),
        ],
        compiler_params=params(),
    )(received, weight, direction, jnp.asarray(xf), jnp.asarray(xi))


def outer_kernel(received, spectra, xf, gradient, curvature, adjoint):
    step = pl.program_id(0)

    @pl.when(step == 0)
    def _():
        adjoint[...] = tall_dot(xf[...], received[...])

    turned = pltpu.roll(spectra[...], C - step * CB, 1)
    pieces = [adjoint[32 * i : 32 * i + 32, :] for i in range(4)]
    for j in range(CB):
        column = jnp.broadcast_to(turned[:, j : j + 1], (64, C))
        real, imag = column[:32], column[32:]
        for s, sink in ((0, gradient), (1, curvature)):
            re, im = pieces[2 * s], pieces[2 * s + 1]
            sink[0, j] = (real * re + imag * im).astype(BF16)
            sink[1, j] = (real * im - imag * re).astype(BF16)


def outer_stage(received, spectra):
    xf = x_forward_table(2, INVERSE_FACTOR)
    moving = pl.BlockSpec((2, CB, 32, C), lambda i: (0, i, 0, 0))
    shape = jax.ShapeDtypeStruct((2, C, 32, C), BF16)
    return pl.pallas_call(
        outer_kernel,
        grid=(C // CB,),
        in_specs=[whole(received.shape), whole(spectra.shape), whole(xf.shape)],
        out_specs=(moving, moving),
        out_shape=(shape, shape),
        scratch_shapes=[pltpu.VMEM((128, C), F32)],
        compiler_params=params(),
    )(received, spectra, jnp.asarray(xf))


def exchange(rows):
    return lax.all_to_all(rows.reshape(2 * NX, -1, C), WIDE, 0, 0, tiled=True).reshape(rows.shape)


def summed(keep, give):
    return keep + lax.ppermute(give, "co", [(0, 1), (1, 0)])


def local(state, target, spectral_weight, direction_weight, inner_weight, outer_weight):
    place = jnp.stack([lax.axis_index(COL), lax.axis_index("co")]).astype(jnp.int32)
    yi, yf = (jnp.asarray(t) for t in y_tables())
    zi, zf = (jnp.asarray(t) for t in z_tables())

    def rows_of(cells):
        return cells[:, 0].transpose(1, 2, 0).reshape(ROWS * NZ, C)

    state_rows = rows_of(state)
    received = exchange(summed(*state_stage(place, state_rows, zf, yf)))
    spectra, planes = mix_stage(received, spectral_weight, direction_weight)
    arrived = exchange(planes.reshape(1024, C))
    other = lax.ppermute(arrived, "co", [(0, 1), (1, 0)])
    weights = (inner_weight, outer_weight)
    keep, give = field_stage(place, arrived, other, state_rows, rows_of(target), weights, (yi, zi, zf, yf))
    adjoint = exchange(summed(keep, give))
    gradient, curvature = outer_stage(adjoint, spectra)
    shape = (2, C, MX, 2, C)
    return gradient.reshape(shape), curvature.reshape(shape)


def solution(mesh):
    fine = Mesh(mesh.devices.reshape(2, 4, 8, 2, 2), GX + COL)
    grid = P(None, GX, COL, None)
    blocks = P(None, None, None, GX + COL, None)
    return jax.shard_map(
        local,
        mesh=fine,
        in_specs=(grid, grid, blocks, blocks, P(), P()),
        out_specs=(blocks, blocks),
        check_vma=False,
    )
```

```python
import math

import jax
import jax.numpy as jnp
import ml_dtypes
import numpy as np
from jax import lax
from jax.experimental import pallas as pl
from jax.experimental.pallas import tpu as pltpu
from jax.sharding import Mesh
from jax.sharding import PartitionSpec as P

C = 128
FF = 512
NX = 64
NY = 128
NZ = 128
MX = 16
MY = 32
MZ = 16
ROWS = 32
COLUMNS = 4
POINTS = NX * NY * NZ
KEPT = MX * MY * MZ
FORWARD_FACTOR = 1.0 / math.sqrt(POINTS)
INVERSE_FACTOR = 2.0 / math.sqrt(KEPT)
LOSS_SCALE = 0.5 * math.sqrt(KEPT / POINTS)
ROWS_A_STEP = 16
CHUNK = ROWS_A_STEP * NZ
CB = 64

GX = ("xl", "y", "z")
COL = ("xh", "co")
WIDE = ("y", "z", "xl", "xh")
F32 = jnp.float32
BF16 = jnp.bfloat16


def params(mebibytes=44):
    return pltpu.CompilerParams(dimension_semantics=("arbitrary",), vmem_limit_bytes=mebibytes * 1024 * 1024)


def signed(number):
    ladder = np.arange(number)
    return np.where(ladder < number // 2, ladder, ladder - number)


def angles(positions, frequencies, length):
    return (np.outer(positions, frequencies) % length) * (2.0 * math.pi / length)


def halves(table):
    high = table.astype(ml_dtypes.bfloat16)
    low = (table - high.astype(np.float64)).astype(ml_dtypes.bfloat16)
    return high, low


def wide(table):
    high, low = halves(table)
    return np.concatenate([high, high, low], axis=-1)


def tall(table):
    high, low = halves(table)
    return np.concatenate([high, low], axis=-2)


def rotation(positions, frequencies, length, sign):
    a = angles(positions, frequencies, length)
    c, s = np.cos(a), sign * np.sin(a)
    return np.stack([np.stack([c, -s]), np.stack([s, c])])


def back_order(column):
    order = []
    for part in range(4):
        xh, co = column // 2 ^ part % 2, column % 2 ^ part // 2
        order += [8 * zh + 4 * xh + 2 * co + m for zh in range(2) for m in range(2)]
    return np.array(order)


def out_order(core):
    order = []
    for part in range(2):
        for zh in range(2):
            for xh in range(2):
                order += [8 * zh + 4 * xh + 2 * (core ^ part) + m for m in range(2)]
    return np.array(order)


def z_tables():
    inverse, forward = [], []
    for column in range(COLUMNS):
        a = angles(np.arange(NZ), back_order(column), NZ)
        inverse.append(wide(np.stack([np.cos(a), -np.sin(a)], -1).reshape(NZ, 2 * MZ)))
    for core in range(2):
        a = angles(np.arange(NZ), out_order(core), NZ)
        high, low = halves(np.stack([np.cos(a), -np.sin(a)], -1).reshape(NZ, 2 * MZ).T)
        forward.append(np.block([[high, high], [low, np.zeros_like(low)]]))
    return np.stack(inverse), np.stack(forward)


def y_tables():
    inverse, forward = [], []
    for column in range(COLUMNS):
        rows = column * ROWS + np.arange(ROWS)
        r = rotation(rows, signed(MY), NY, 1.0)
        inverse.append(wide(r.transpose(0, 2, 1, 3).reshape(2 * ROWS, 2 * MY)))
        r = rotation(rows, signed(MY), NY, -1.0)
        forward.append(wide(r.transpose(0, 3, 1, 2).reshape(2 * MY, 2 * ROWS)))
    return np.stack(inverse), np.stack(forward)


def x_places():
    return np.arange(NX).reshape(2, 4, 8).transpose(1, 2, 0).reshape(NX)


def x_forward_table(fields, factor):
    r = rotation(x_places(), signed(MX), NX, -1.0) * factor
    t = np.zeros((fields, 2, MX, 2, NX, 2, 2, fields, 2))
    for s in range(fields):
        for m in range(2):
            for xh in range(2):
                t[s, :, :, m, :, xh, m, s, :] = r.transpose(0, 3, 2, 1)
    return tall(t.reshape(fields * 2 * MX * 2, NX * 2 * 2 * fields * 2))


def x_inverse_table(factor):
    r = rotation(x_places(), signed(MX), NX, 1.0) * factor
    t = np.zeros((NX, 2, 2, 2, 2, 2, MX, 2))
    for s in range(2):
        for m in range(2):
            t[:, m, s, :, s, :, :, m] = r.transpose(2, 0, 1, 3)
    return wide(t.reshape(NX * 8, 128))


def dot(a, b):
    return jnp.dot(a, b, preferred_element_type=F32)


def two(values):
    high = values.astype(BF16)
    return high, (values - high.astype(F32)).astype(BF16)


def three(values):
    high, low = two(values)
    return jnp.concatenate([high, low, high], axis=0)


def tall_dot(table, values):
    rows = table.shape[0] // 2
    high, low = two(values)
    first = dot(table, high)
    return first[:rows] + first[rows:] + dot(table[:rows], low)


def mode_rows(k, extra):
    zh, xh, m = k % 8 // 4, k % 4 // 2, k % 2
    return [pl.ds(zh * 32 + xl * 16 + xh * 8 + m * 4 + extra, 16, stride=64) for xl in range(2)]


def back_rows(k, extra):
    zh, m = k % 4 // 2, k % 2
    return [pl.ds(zh * 16 + xl * 8 + m * 4 + extra, 16, stride=32) for xl in range(2)]


def state_rows_of(k, extra):
    zh, xh, m = k % 8 // 4, k % 4 // 2, k % 2
    return [pl.ds(zh * 16 + xl * 8 + xh * 4 + m * 2 + extra, 16, stride=32) for xl in range(2)]


def rows_forward(values, fields, table, after, y):
    rows = dot(table, jnp.concatenate(two(values), axis=0))
    rows = rows[: 2 * MZ] + rows[2 * MZ :]
    start = pl.multiple_of(y * 2 * MZ, 2 * MZ)
    for s in range(fields):
        after[s, pl.ds(start, 2 * MZ), :] = rows[:, s * C : (s + 1) * C]


def columns_forward(fields, table, after, keep, give):
    pieces = [(k, s) for k in range(MZ) for s in range(fields)]
    for pair in zip(pieces[::2], pieces[1::2]):
        parts = []
        for k, s in pair:
            q = [after[s, pl.ds(2 * k + i, ROWS, stride=2 * MZ), :] for i in range(2)]
            parts.append(jnp.concatenate(q, axis=0))
        rows = dot(table, three(jnp.concatenate(parts, axis=1)))
        for i, (k, s) in enumerate(pair):
            sink = keep if k < 8 else give
            for r in range(2):
                places = mode_rows(k, 2 * s + r) if fields == 2 else state_rows_of(k, r)
                for xl, place in enumerate(places):
                    at = r * MY + xl * 16
                    sink[place, :] = rows[at : at + 16, i * C : (i + 1) * C]


def state_kernel(place, state, zf, yf, keep, give, after):
    for y in range(0, ROWS, 2):
        pair = jnp.concatenate([state[(y + i) * NZ : (y + i + 1) * NZ] for i in range(2)], axis=1)
        rows = dot(zf[0, :, :NZ], pair)
        rows = rows[: 2 * MZ] + rows[2 * MZ :]
        for i in range(2):
            after[0, pl.ds((y + i) * 2 * MZ, 2 * MZ), :] = rows[:, i * C : (i + 1) * C]
    columns_forward(1, yf[0], after, keep, give)


def ready_kernel(place, w1_, w2_, yi_, zi_, zf_, yf_, w1, w2, w1t, w2t, yi, zi, zf, yf):
    w1[...] = w1_[...]
    w2[...] = w2_[...]
    w1t[...] = w1_[...].T
    w2t[...] = w2_[...].T
    yi[...] = yi_[0]
    zi[...] = zi_[0]
    zf[...] = zf_[0]
    yf[...] = yf_[0]


def field_kernel(
    q00, q10, q01, q11, state, target, w1, w2, w1t, w2t, yi, zi, zf, yf, keep, give, half, after
):
    step = pl.program_id(0)

    @pl.when(step == 0)
    def _():
        for k in range(MZ):
            source = (q00, q10, q01, q11)[k // 4]
            parts = []
            for s in range(2):
                p = [source[place, :] for i in range(2) for place in back_rows(k, 2 * s + i)]
                parts.append(jnp.concatenate(p, axis=0))
            rows = dot(yi[...], three(jnp.concatenate(parts, axis=1)))
            for s in range(2):
                half[s, pl.ds(k * 64, 64), :] = rows[:, s * C : (s + 1) * C]

    first = step * ROWS_A_STEP
    fields = []
    for i in range(ROWS_A_STEP):
        taken = [half[s, pl.ds(first + i, 2 * MZ, stride=ROWS), :] for s in range(2)]
        fields.append(dot(zi[...], three(jnp.concatenate(taken, axis=1))))
    fields = jnp.concatenate(fields, axis=0).astype(BF16)
    primal, tangent = fields[:, :C], fields[:, C:]
    layer_input = state[...].astype(F32) + primal.astype(F32)
    hidden = dot(layer_input.astype(BF16), w1[...])
    mass = 0.5 * (1.0 + lax.erf(hidden * math.sqrt(0.5)))
    density = jnp.exp(-0.5 * hidden * hidden) * (1.0 / math.sqrt(2.0 * math.pi))
    slope = mass + hidden * density
    activation = (hidden * mass).astype(BF16)
    seed_primal = LOSS_SCALE * (layer_input + dot(activation, w2[...]) - target[...].astype(F32))
    hidden_tangent = dot(tangent, w1[...])
    activation_tangent = (slope * hidden_tangent).astype(BF16)
    seed_tangent = LOSS_SCALE * (tangent.astype(F32) + dot(activation_tangent, w2[...]))
    back_primal = dot(seed_primal.astype(BF16), w2t[...])
    back_tangent = dot(seed_tangent.astype(BF16), w2t[...])
    delta_primal = (slope * back_primal).astype(BF16)
    bend = density * (2.0 - hidden * hidden)
    delta_tangent = (bend * hidden_tangent * back_primal + slope * back_tangent).astype(BF16)
    cotangents = [seed_primal + dot(delta_primal, w1t[...]), seed_tangent + dot(delta_tangent, w1t[...])]
    cotangents = jnp.concatenate(cotangents, axis=1)
    for i in range(ROWS_A_STEP):
        rows_forward(cotangents[i * NZ : (i + 1) * NZ], 2, zf[...], after, first + i)

    @pl.when(step == ROWS // ROWS_A_STEP - 1)
    def _():
        columns_forward(2, yf[...], after, keep, give)


def whole(shape):
    return pl.BlockSpec(shape, lambda i: (0,) * len(shape))


def still(shape):
    return pl.BlockSpec(shape, lambda i, place: (0,) * len(shape))


def picked(table, index):
    return pl.BlockSpec((1,) + table.shape[1:], lambda i, place: (place[index], 0, 0))


def state_stage(place, state, zf, yf):
    shape = jax.ShapeDtypeStruct((512, C), F32)
    return pl.pallas_call(
        state_kernel,
        grid_spec=pltpu.PrefetchScalarGridSpec(
            num_scalar_prefetch=1,
            grid=(1,),
            in_specs=[still(state.shape), picked(zf, 1), picked(yf, 0)],
            out_specs=(still((512, C)), still((512, C))),
            scratch_shapes=[pltpu.VMEM((1, 1024, C), F32)],
        ),
        out_shape=(shape, shape),
        compiler_params=params(),
    )(place, state, zf, yf)


def ready_stage(place, w1, w2, tables):
    shapes = [(C, FF), (FF, C), (FF, C), (C, FF)] + [t.shape[1:] for t in tables]
    return pl.pallas_call(
        ready_kernel,
        grid_spec=pltpu.PrefetchScalarGridSpec(
            num_scalar_prefetch=1,
            grid=(1,),
            in_specs=[still(w1.shape), still(w2.shape)] + [picked(t, i) for t, i in zip(tables, (0, 0, 1, 0))],
            out_specs=tuple(still(shape) for shape in shapes),
        ),
        out_shape=tuple(jax.ShapeDtypeStruct(shape, BF16) for shape in shapes),
        compiler_params=params(16),
    )(place, w1, w2, *tables)


def field_stage(quarters, state, target, ready):
    moving = pl.BlockSpec((CHUNK, C), lambda i: (i, 0))
    shape = jax.ShapeDtypeStruct((1024, C), F32)
    return pl.pallas_call(
        field_kernel,
        grid=(ROWS // ROWS_A_STEP,),
        in_specs=[whole((512, C))] * 4 + [moving] * 2 + [whole(r.shape) for r in ready],
        out_specs=(whole((1024, C)), whole((1024, C))),
        out_shape=(shape, shape),
        scratch_shapes=[pltpu.VMEM((2, 1024, C), F32), pltpu.VMEM((2, 1024, C), F32)],
        compiler_params=params(),
    )(*quarters, state, target, *ready)


def mix_kernel(received, weight, direction, xf, xi_, spectra, planes, total, xi, arrival):
    step = pl.program_id(0)
    second = pltpu.make_async_copy(xi_, xi, arrival)

    @pl.when(step == 0)
    def _():
        second.start()
        spectra[...] = tall_dot(xf[...], received[...])
        total[...] = jnp.zeros_like(total)

    turned = pltpu.roll(spectra[...], C - step * CB, 1)
    sums = [total[i] for i in range(4)]
    for j in range(CB):
        column = jnp.broadcast_to(turned[:, j : j + 1], (64, C))
        real, imag = column[:32], column[32:]
        for s, w in ((0, weight), (1, direction)):
            wr, wi = w[0, j].astype(F32), w[1, j].astype(F32)
            sums[2 * s] = sums[2 * s] + (wr * real - wi * imag)
            sums[2 * s + 1] = sums[2 * s + 1] + (wr * imag + wi * real)
    for i in range(4):
        total[i] = sums[i]

    @pl.when(step == C // CB - 1)
    def _():
        second.wait()
        out = dot(xi[...], three(jnp.concatenate(sums, axis=0)))
        planes[...] = out


def mix_stage(received, weight, direction):
    xf = x_forward_table(1, FORWARD_FACTOR)
    xi = x_inverse_table(INVERSE_FACTOR)
    weight = weight.reshape(2, C, 32, C)
    direction = direction.reshape(2, C, 32, C)
    moving = pl.BlockSpec((2, CB, 32, C), lambda i: (0, i, 0, 0))
    return pl.pallas_call(
        mix_kernel,
        grid=(C // CB,),
        in_specs=[whole(received.shape), moving, moving, whole(xf.shape), pl.BlockSpec(memory_space=pltpu.HBM)],
        out_specs=(whole((64, C)), whole((NX * 8, C))),
        out_shape=(jax.ShapeDtypeStruct((64, C), F32), jax.ShapeDtypeStruct((NX * 8, C), F32)),
        scratch_shapes=[
            pltpu.VMEM((4, 32, C), F32),
            pltpu.VMEM(xi.shape, BF16),
            pltpu.SemaphoreType.DMA,
        ],
        compiler_params=params(),
    )(received, weight, direction, jnp.asarray(xf), pltpu.with_memory_space_constraint(jnp.asarray(xi), pltpu.HBM))


def outer_kernel(received, spectra, xf, gradient, curvature, adjoint):
    step = pl.program_id(0)

    @pl.when(step == 0)
    def _():
        adjoint[...] = tall_dot(xf[...], received[...])

    turned = pltpu.roll(spectra[...], C - step * CB, 1)
    pieces = [adjoint[32 * i : 32 * i + 32, :] for i in range(4)]
    for j in range(CB):
        column = jnp.broadcast_to(turned[:, j : j + 1], (64, C))
        real, imag = column[:32], column[32:]
        for s, sink in ((0, gradient), (1, curvature)):
            re, im = pieces[2 * s], pieces[2 * s + 1]
            sink[0, j] = (real * re + imag * im).astype(BF16)
            sink[1, j] = (real * im - imag * re).astype(BF16)


def outer_stage(received, spectra):
    xf = x_forward_table(2, INVERSE_FACTOR)
    moving = pl.BlockSpec((2, CB, 32, C), lambda i: (0, i, 0, 0))
    shape = jax.ShapeDtypeStruct((2, C, 32, C), BF16)
    return pl.pallas_call(
        outer_kernel,
        grid=(C // CB,),
        in_specs=[whole(received.shape), whole(spectra.shape), whole(xf.shape)],
        out_specs=(moving, moving),
        out_shape=(shape, shape),
        scratch_shapes=[pltpu.VMEM((128, C), F32)],
        compiler_params=params(),
    )(received, spectra, jnp.asarray(xf))


def exchange(rows, group):
    size = lax.axis_size(group)
    return lax.all_to_all(rows.reshape(size, -1, C), group, 0, 0, tiled=True).reshape(rows.shape)


def swap(rows, axis):
    return lax.ppermute(rows, axis, [(0, 1), (1, 0)])


def local(state, target, spectral_weight, direction_weight, inner_weight, outer_weight):
    place = jnp.stack([lax.axis_index(COL), lax.axis_index("co")]).astype(jnp.int32)
    yi, yf = (jnp.asarray(t) for t in y_tables())
    zi, zf = (jnp.asarray(t) for t in z_tables())

    def rows_of(cells):
        return cells[:, 0].transpose(1, 2, 0).reshape(ROWS * NZ, C)

    state_rows = rows_of(state)
    keep, give = state_stage(place, state_rows, zf, yf)
    received = exchange(keep + swap(give, "co"), WIDE)
    spectra, planes = mix_stage(received, spectral_weight, direction_weight)
    q00 = exchange(planes, WIDE[:3])
    q10 = swap(q00, "xh")
    q01 = swap(q00, "co")
    q00, target, w1, w2 = lax.optimization_barrier((q00, target, inner_weight, outer_weight))
    ready = ready_stage(place, w1, w2, (yi, zi, zf, yf))
    target_rows = rows_of(target)
    q10, ready, target_rows = lax.optimization_barrier((q10, ready, target_rows))
    q11 = swap(q10, "co")
    keep, give = field_stage((q00, q10, q01, q11), state_rows, target_rows, ready)
    adjoint = exchange(keep + swap(give, "co"), WIDE)
    gradient, curvature = outer_stage(adjoint, spectra)
    shape = (2, C, MX, 2, C)
    return gradient.reshape(shape), curvature.reshape(shape)


def solution(mesh):
    fine = Mesh(mesh.devices.reshape(2, 4, 8, 2, 2), GX + COL)
    grid = P(None, GX, COL, None)
    blocks = P(None, None, None, GX + COL, None)
    return jax.shard_map(
        local,
        mesh=fine,
        in_specs=(grid, grid, blocks, blocks, P(), P()),
        out_specs=(blocks, blocks),
        check_vma=False,
    )
```

```python
import math

import jax
import jax.numpy as jnp
import ml_dtypes
import numpy as np
from jax import lax
from jax.experimental import pallas as pl
from jax.experimental.pallas import tpu as pltpu
from jax.sharding import Mesh
from jax.sharding import PartitionSpec as P

C = 128
FF = 512
NX = 64
NY = 128
NZ = 128
MX = 16
MY = 32
MZ = 16
ROWS = 32
COLUMNS = 4
POINTS = NX * NY * NZ
KEPT = MX * MY * MZ
FORWARD_FACTOR = 1.0 / math.sqrt(POINTS)
INVERSE_FACTOR = 2.0 / math.sqrt(KEPT)
LOSS_SCALE = 0.5 * math.sqrt(KEPT / POINTS)
ROWS_A_STEP = 16
CHUNK = ROWS_A_STEP * NZ
CB = 64
MB = 32

GX = ("xl", "y", "z")
COL = ("xh", "co")
WIDE = ("y", "z", "xl", "xh")
F32 = jnp.float32
BF16 = jnp.bfloat16


def params(mebibytes=44):
    return pltpu.CompilerParams(dimension_semantics=("arbitrary",), vmem_limit_bytes=mebibytes * 1024 * 1024)


def signed(number):
    ladder = np.arange(number)
    return np.where(ladder < number // 2, ladder, ladder - number)


def angles(positions, frequencies, length):
    return (np.outer(positions, frequencies) % length) * (2.0 * math.pi / length)


def halves(table):
    high = table.astype(ml_dtypes.bfloat16)
    low = (table - high.astype(np.float64)).astype(ml_dtypes.bfloat16)
    return high, low


def wide(table):
    high, low = halves(table)
    return np.concatenate([high, high, low], axis=-1)


def tall(table):
    high, low = halves(table)
    return np.concatenate([high, low], axis=-2)


def rotation(positions, frequencies, length, sign):
    a = angles(positions, frequencies, length)
    c, s = np.cos(a), sign * np.sin(a)
    return np.stack([np.stack([c, -s]), np.stack([s, c])])


def back_order(column):
    order = []
    for part in range(4):
        xh, co = column // 2 ^ part % 2, column % 2 ^ part // 2
        order += [8 * zh + 4 * xh + 2 * co + m for zh in range(2) for m in range(2)]
    return np.array(order)


def out_order(core):
    order = []
    for part in range(2):
        for zh in range(2):
            for xh in range(2):
                order += [8 * zh + 4 * xh + 2 * (core ^ part) + m for m in range(2)]
    return np.array(order)


def z_tables():
    inverse, forward = [], []
    for column in range(COLUMNS):
        a = angles(np.arange(NZ), back_order(column), NZ)
        inverse.append(wide(np.stack([np.cos(a), -np.sin(a)], -1).reshape(NZ, 2 * MZ)))
    for core in range(2):
        a = angles(np.arange(NZ), out_order(core), NZ)
        high, low = halves(np.stack([np.cos(a), -np.sin(a)], -1).reshape(NZ, 2 * MZ).T)
        forward.append(np.block([[high, high], [low, np.zeros_like(low)]]))
    return np.stack(inverse), np.stack(forward)


def y_tables():
    inverse, forward = [], []
    for column in range(COLUMNS):
        rows = column * ROWS + np.arange(ROWS)
        r = rotation(rows, signed(MY), NY, 1.0)
        inverse.append(wide(r.transpose(0, 2, 1, 3).reshape(2 * ROWS, 2 * MY)))
        r = rotation(rows, signed(MY), NY, -1.0)
        forward.append(wide(r.transpose(0, 3, 1, 2).reshape(2 * MY, 2 * ROWS)))
    return np.stack(inverse), np.stack(forward)


def x_places():
    return np.arange(NX).reshape(2, 4, 8).transpose(1, 2, 0).reshape(NX)


def x_forward_table(fields, factor):
    r = rotation(x_places(), signed(MX), NX, -1.0) * factor
    t = np.zeros((fields, 2, MX, 2, NX, 2, 2, fields, 2))
    for s in range(fields):
        for m in range(2):
            for xh in range(2):
                t[s, :, :, m, :, xh, m, s, :] = r.transpose(0, 3, 2, 1)
    return tall(t.reshape(fields * 2 * MX * 2, NX * 2 * 2 * fields * 2))


def x_inverse_table(factor):
    r = rotation(x_places(), signed(MX), NX, 1.0) * factor
    t = np.zeros((NX, 2, 2, 2, 2, 2, MX, 2))
    for s in range(2):
        for m in range(2):
            t[:, m, s, :, s, :, :, m] = r.transpose(2, 0, 1, 3)
    return wide(t.reshape(NX * 8, 128))


def dot(a, b):
    return jnp.dot(a, b, preferred_element_type=F32)


def two(values):
    high = values.astype(BF16)
    return high, (values - high.astype(F32)).astype(BF16)


def three(values):
    high, low = two(values)
    return jnp.concatenate([high, low, high], axis=0)


def tall_dot(table, values):
    rows = table.shape[0] // 2
    high, low = two(values)
    first = dot(table, high)
    return first[:rows] + first[rows:] + dot(table[:rows], low)


def mode_rows(k, extra):
    zh, xh, m = k % 8 // 4, k % 4 // 2, k % 2
    return [pl.ds(zh * 32 + xl * 16 + xh * 8 + m * 4 + extra, 16, stride=64) for xl in range(2)]


def back_rows(k, extra):
    zh, m = k % 4 // 2, k % 2
    return [pl.ds(zh * 16 + xl * 8 + m * 4 + extra, 16, stride=32) for xl in range(2)]


def state_rows_of(k, extra):
    zh, xh, m = k % 8 // 4, k % 4 // 2, k % 2
    return [pl.ds(zh * 16 + xl * 8 + xh * 4 + m * 2 + extra, 16, stride=32) for xl in range(2)]


def rows_forward(values, fields, table, after, y):
    rows = dot(table, jnp.concatenate(two(values), axis=0))
    rows = rows[: 2 * MZ] + rows[2 * MZ :]
    start = pl.multiple_of(y * 2 * MZ, 2 * MZ)
    for s in range(fields):
        after[s, pl.ds(start, 2 * MZ), :] = rows[:, s * C : (s + 1) * C]


def columns_forward(fields, table, after, keep, give):
    pieces = [(k, s) for k in range(MZ) for s in range(fields)]
    for pair in zip(pieces[::2], pieces[1::2]):
        parts = []
        for k, s in pair:
            q = [after[s, pl.ds(2 * k + i, ROWS, stride=2 * MZ), :] for i in range(2)]
            parts.append(jnp.concatenate(q, axis=0))
        rows = dot(table, three(jnp.concatenate(parts, axis=1)))
        for i, (k, s) in enumerate(pair):
            sink = keep if k < 8 else give
            for r in range(2):
                places = mode_rows(k, 2 * s + r) if fields == 2 else state_rows_of(k, r)
                for xl, place in enumerate(places):
                    at = r * MY + xl * 16
                    sink[place, :] = rows[at : at + 16, i * C : (i + 1) * C]


def state_kernel(place, state, zf, yf, keep, give, after):
    planes = jnp.transpose(state[...], (1, 0, 2))
    for y in range(0, ROWS, 2):
        pair = planes[y : y + 2].reshape(2 * C, NZ)
        rows = lax.dot_general(zf[0, :, :NZ], pair, (((1,), (1,)), ((), ())), preferred_element_type=F32)
        rows = rows[: 2 * MZ] + rows[2 * MZ :]
        for i in range(2):
            after[0, pl.ds((y + i) * 2 * MZ, 2 * MZ), :] = rows[:, i * C : (i + 1) * C]
    columns_forward(1, yf[0], after, keep, give)


def ready_kernel(place, w1_, w2_, yi_, zi_, zf_, yf_, w1, w2, w1t, w2t, yi, zi, zf, yf):
    w1[...] = w1_[...]
    w2[...] = w2_[...]
    w1t[...] = w1_[...].T
    w2t[...] = w2_[...].T
    yi[...] = yi_[0]
    zi[...] = zi_[0]
    zf[...] = zf_[0]
    yf[...] = yf_[0]


def field_kernel(
    q00, q10, q01, q11, state, target, w1, w2, w1t, w2t, yi, zi, zf, yf, keep, give, half, after
):
    step = pl.program_id(0)

    @pl.when(step == 0)
    def _():
        for k in range(MZ):
            source = (q00, q10, q01, q11)[k // 4]
            parts = []
            for s in range(2):
                p = [source[place, :] for i in range(2) for place in back_rows(k, 2 * s + i)]
                parts.append(jnp.concatenate(p, axis=0))
            rows = dot(yi[...], three(jnp.concatenate(parts, axis=1)))
            for s in range(2):
                half[s, pl.ds(k * 64, 64), :] = rows[:, s * C : (s + 1) * C]

    first = step * ROWS_A_STEP
    fields = []
    for i in range(ROWS_A_STEP):
        taken = [half[s, pl.ds(first + i, 2 * MZ, stride=ROWS), :] for s in range(2)]
        fields.append(dot(zi[...], three(jnp.concatenate(taken, axis=1))))
    fields = jnp.concatenate(fields, axis=0).astype(BF16)
    primal, tangent = fields[:, :C], fields[:, C:]
    layer_input = state[...].astype(F32) + primal.astype(F32)
    hidden = dot(layer_input.astype(BF16), w1[...])
    mass = 0.5 * (1.0 + lax.erf(hidden * math.sqrt(0.5)))
    density = jnp.exp(-0.5 * hidden * hidden) * (1.0 / math.sqrt(2.0 * math.pi))
    slope = mass + hidden * density
    activation = (hidden * mass).astype(BF16)
    seed_primal = LOSS_SCALE * (layer_input + dot(activation, w2[...]) - target[...].astype(F32))
    hidden_tangent = dot(tangent, w1[...])
    activation_tangent = (slope * hidden_tangent).astype(BF16)
    seed_tangent = LOSS_SCALE * (tangent.astype(F32) + dot(activation_tangent, w2[...]))
    back_primal = dot(seed_primal.astype(BF16), w2t[...])
    back_tangent = dot(seed_tangent.astype(BF16), w2t[...])
    delta_primal = (slope * back_primal).astype(BF16)
    bend = density * (2.0 - hidden * hidden)
    delta_tangent = (bend * hidden_tangent * back_primal + slope * back_tangent).astype(BF16)
    cotangents = [seed_primal + dot(delta_primal, w1t[...]), seed_tangent + dot(delta_tangent, w1t[...])]
    cotangents = jnp.concatenate(cotangents, axis=1)
    for i in range(ROWS_A_STEP):
        rows_forward(cotangents[i * NZ : (i + 1) * NZ], 2, zf[...], after, first + i)

    @pl.when(step == ROWS // ROWS_A_STEP - 1)
    def _():
        columns_forward(2, yf[...], after, keep, give)


def whole(shape):
    return pl.BlockSpec(shape, lambda i: (0,) * len(shape))


def still(shape):
    return pl.BlockSpec(shape, lambda i, place: (0,) * len(shape))


def picked(table, index):
    return pl.BlockSpec((1,) + table.shape[1:], lambda i, place: (place[index], 0, 0))


def state_stage(place, state, zf, yf):
    shape = jax.ShapeDtypeStruct((512, C), F32)
    return pl.pallas_call(
        state_kernel,
        grid_spec=pltpu.PrefetchScalarGridSpec(
            num_scalar_prefetch=1,
            grid=(1,),
            in_specs=[still(state.shape), picked(zf, 1), picked(yf, 0)],
            out_specs=(still((512, C)), still((512, C))),
            scratch_shapes=[pltpu.VMEM((1, 1024, C), F32)],
        ),
        out_shape=(shape, shape),
        compiler_params=params(16),
    )(place, state, zf, yf)


def ready_stage(place, w1, w2, tables):
    shapes = [(C, FF), (FF, C), (FF, C), (C, FF)] + [t.shape[1:] for t in tables]
    return pl.pallas_call(
        ready_kernel,
        grid_spec=pltpu.PrefetchScalarGridSpec(
            num_scalar_prefetch=1,
            grid=(1,),
            in_specs=[still(w1.shape), still(w2.shape)] + [picked(t, i) for t, i in zip(tables, (0, 0, 1, 0))],
            out_specs=tuple(still(shape) for shape in shapes),
        ),
        out_shape=tuple(jax.ShapeDtypeStruct(shape, BF16) for shape in shapes),
        compiler_params=params(16),
    )(place, w1, w2, *tables)


def field_stage(quarters, state, target, ready):
    moving = pl.BlockSpec((CHUNK, C), lambda i: (i, 0))
    shape = jax.ShapeDtypeStruct((1024, C), F32)
    return pl.pallas_call(
        field_kernel,
        grid=(ROWS // ROWS_A_STEP,),
        in_specs=[whole((512, C))] * 4 + [moving] * 2 + [whole(r.shape) for r in ready],
        out_specs=(whole((1024, C)), whole((1024, C))),
        out_shape=(shape, shape),
        scratch_shapes=[pltpu.VMEM((2, 1024, C), F32), pltpu.VMEM((2, 1024, C), F32)],
        compiler_params=params(),
    )(*quarters, state, target, *ready)


def mix_kernel(received, weight, direction, xf, xi_, spectra, planes, held, xi, arrivals, arrival):
    last = pltpu.make_async_copy(xi_, xi, arrival)
    copies = []
    for i in range(C // MB):
        at = pl.ds(i * MB, MB)
        for s, source in ((0, weight), (1, direction)):
            copies.append(pltpu.make_async_copy(source.at[:, at], held.at[s, :, at], arrivals.at[2 * i + s]))
    for copy in copies:
        copy.start()
    last.start()
    modes = tall_dot(xf[...], received[...])
    spectra[...] = modes
    sums = [jnp.zeros((32, C), F32) for i in range(4)]
    for j in range(C):
        if j % MB == 0:
            copies[2 * (j // MB)].wait()
            copies[2 * (j // MB) + 1].wait()
        column = jnp.broadcast_to(modes[:, j : j + 1], (64, C))
        real, imag = column[:32], column[32:]
        for s in range(2):
            wr, wi = held[s, 0, j].astype(F32), held[s, 1, j].astype(F32)
            sums[2 * s] = sums[2 * s] + (wr * real - wi * imag)
            sums[2 * s + 1] = sums[2 * s + 1] + (wr * imag + wi * real)
    last.wait()
    planes[...] = dot(xi[...], three(jnp.concatenate(sums, axis=0)))


def mix_stage(received, weight, direction):
    xf = x_forward_table(1, FORWARD_FACTOR)
    xi = x_inverse_table(INVERSE_FACTOR)
    far = pl.BlockSpec(memory_space=pltpu.HBM)

    def stay(array):
        return pltpu.with_memory_space_constraint(array, pltpu.HBM)

    return pl.pallas_call(
        mix_kernel,
        grid=(1,),
        in_specs=[whole(received.shape), far, far, whole(xf.shape), far],
        out_specs=(whole((64, C)), whole((NX * 8, C))),
        out_shape=(jax.ShapeDtypeStruct((64, C), F32), jax.ShapeDtypeStruct((NX * 8, C), F32)),
        scratch_shapes=[
            pltpu.VMEM((2, 2, C, 32, C), BF16),
            pltpu.VMEM(xi.shape, BF16),
            pltpu.SemaphoreType.DMA((2 * (C // MB),)),
            pltpu.SemaphoreType.DMA,
        ],
        compiler_params=params(16),
    )(
        received,
        stay(weight.reshape(2, C, 32, C)),
        stay(direction.reshape(2, C, 32, C)),
        jnp.asarray(xf),
        stay(jnp.asarray(xi)),
    )


def outer_kernel(received, spectra, xf, gradient, curvature, adjoint):
    step = pl.program_id(0)

    @pl.when(step == 0)
    def _():
        adjoint[...] = tall_dot(xf[...], received[...])

    turned = pltpu.roll(spectra[...], C - step * CB, 1)
    pieces = [adjoint[32 * i : 32 * i + 32, :] for i in range(4)]
    for j in range(CB):
        column = jnp.broadcast_to(turned[:, j : j + 1], (64, C))
        real, imag = column[:32], column[32:]
        for s, sink in ((0, gradient), (1, curvature)):
            re, im = pieces[2 * s], pieces[2 * s + 1]
            sink[0, j] = (real * re + imag * im).astype(BF16)
            sink[1, j] = (real * im - imag * re).astype(BF16)


def outer_stage(received, spectra):
    xf = x_forward_table(2, INVERSE_FACTOR)
    moving = pl.BlockSpec((2, CB, 32, C), lambda i: (0, i, 0, 0))
    shape = jax.ShapeDtypeStruct((2, C, 32, C), BF16)
    return pl.pallas_call(
        outer_kernel,
        grid=(C // CB,),
        in_specs=[whole(received.shape), whole(spectra.shape), whole(xf.shape)],
        out_specs=(moving, moving),
        out_shape=(shape, shape),
        scratch_shapes=[pltpu.VMEM((128, C), F32)],
        compiler_params=params(24),
    )(received, spectra, jnp.asarray(xf))


def exchange(rows, group):
    size = lax.axis_size(group)
    return lax.all_to_all(rows.reshape(size, -1, C), group, 0, 0, tiled=True).reshape(rows.shape)


def swap(rows, axis):
    return lax.ppermute(rows, axis, [(0, 1), (1, 0)])


def local(state, target, spectral_weight, direction_weight, inner_weight, outer_weight):
    place = jnp.stack([lax.axis_index(COL), lax.axis_index("co")]).astype(jnp.int32)
    yi, yf = (jnp.asarray(t) for t in y_tables())
    zi, zf = (jnp.asarray(t) for t in z_tables())

    def rows_of(cells):
        return cells[:, 0].transpose(1, 2, 0).reshape(ROWS * NZ, C)

    keep, give = state_stage(place, state.reshape(C, ROWS, NZ), zf, yf)
    received = exchange(keep + swap(give, "co"), WIDE)
    spectra, planes = mix_stage(received, spectral_weight, direction_weight)
    q00 = exchange(planes, WIDE[:3])
    q10 = swap(q00, "xh")
    q01 = swap(q00, "co")
    q00, state, target, w1, w2 = lax.optimization_barrier((q00, state, target, inner_weight, outer_weight))
    ready = ready_stage(place, w1, w2, (yi, zi, zf, yf))
    rows = rows_of(state), rows_of(target)
    q10, ready, rows = lax.optimization_barrier((q10, ready, rows))
    q11 = swap(q10, "co")
    keep, give = field_stage((q00, q10, q01, q11), *rows, ready)
    adjoint = exchange(keep + swap(give, "co"), WIDE)
    gradient, curvature = outer_stage(adjoint, spectra)
    shape = (2, C, MX, 2, C)
    return gradient.reshape(shape), curvature.reshape(shape)


def solution(mesh):
    fine = Mesh(mesh.devices.reshape(2, 4, 8, 2, 2), GX + COL)
    grid = P(None, GX, COL, None)
    blocks = P(None, None, None, GX + COL, None)
    return jax.shard_map(
        local,
        mesh=fine,
        in_specs=(grid, grid, blocks, blocks, P(), P()),
        out_specs=(blocks, blocks),
        check_vma=False,
    )
```

```python
import math

import jax
import jax.numpy as jnp
import ml_dtypes
import numpy as np
from jax import lax
from jax.experimental import pallas as pl
from jax.experimental.pallas import tpu as pltpu
from jax.sharding import Mesh
from jax.sharding import PartitionSpec as P

C = 128
FF = 512
NX = 64
NY = 128
NZ = 128
MX = 16
MY = 32
MZ = 16
ROWS = 32
COLUMNS = 4
POINTS = NX * NY * NZ
KEPT = MX * MY * MZ
FORWARD_FACTOR = 1.0 / math.sqrt(POINTS)
INVERSE_FACTOR = 2.0 / math.sqrt(KEPT)
LOSS_SCALE = 0.5 * math.sqrt(KEPT / POINTS)
ROWS_A_STEP = 16
CHUNK = ROWS_A_STEP * NZ
CB = 64
PIECES = 4

GX = ("xl", "y", "z")
COL = ("xh", "co")
WIDE = ("y", "z", "xl", "xh")
F32 = jnp.float32
BF16 = jnp.bfloat16


def params(mebibytes=44):
    return pltpu.CompilerParams(dimension_semantics=("arbitrary",), vmem_limit_bytes=mebibytes * 1024 * 1024)


def signed(number):
    ladder = np.arange(number)
    return np.where(ladder < number // 2, ladder, ladder - number)


def angles(positions, frequencies, length):
    return (np.outer(positions, frequencies) % length) * (2.0 * math.pi / length)


def halves(table):
    high = table.astype(ml_dtypes.bfloat16)
    low = (table - high.astype(np.float64)).astype(ml_dtypes.bfloat16)
    return high, low


def wide(table):
    high, low = halves(table)
    return np.concatenate([high, high, low], axis=-1)


def tall(table):
    high, low = halves(table)
    return np.concatenate([high, low], axis=-2)


def rotation(positions, frequencies, length, sign):
    a = angles(positions, frequencies, length)
    c, s = np.cos(a), sign * np.sin(a)
    return np.stack([np.stack([c, -s]), np.stack([s, c])])


def back_order(column):
    order = []
    for part in range(4):
        xh, co = column // 2 ^ part % 2, column % 2 ^ part // 2
        order += [8 * zh + 4 * xh + 2 * co + m for zh in range(2) for m in range(2)]
    return np.array(order)


def out_order(core):
    order = []
    for part in range(2):
        for zh in range(2):
            for xh in range(2):
                order += [8 * zh + 4 * xh + 2 * (core ^ part) + m for m in range(2)]
    return np.array(order)


def z_tables():
    inverse, forward = [], []
    for column in range(COLUMNS):
        a = angles(np.arange(NZ), back_order(column), NZ)
        inverse.append(wide(np.stack([np.cos(a), -np.sin(a)], -1).reshape(NZ, 2 * MZ)))
    for core in range(2):
        a = angles(np.arange(NZ), out_order(core), NZ)
        high, low = halves(np.stack([np.cos(a), -np.sin(a)], -1).reshape(NZ, 2 * MZ).T)
        forward.append(np.block([[high, high], [low, np.zeros_like(low)]]))
    return np.stack(inverse), np.stack(forward)


def y_tables():
    inverse, forward = [], []
    for column in range(COLUMNS):
        rows = column * ROWS + np.arange(ROWS)
        r = rotation(rows, signed(MY), NY, 1.0)
        inverse.append(wide(r.transpose(0, 2, 1, 3).reshape(2 * ROWS, 2 * MY)))
        r = rotation(rows, signed(MY), NY, -1.0)
        forward.append(wide(r.transpose(0, 3, 1, 2).reshape(2 * MY, 2 * ROWS)))
    return np.stack(inverse), np.stack(forward)


def x_places():
    return np.arange(NX).reshape(2, 4, 8).transpose(1, 2, 0).reshape(NX)


def x_forward_table(fields, factor):
    r = rotation(x_places(), signed(MX), NX, -1.0) * factor
    t = np.zeros((fields, 2, MX, 2, NX, 2, 2, fields, 2))
    for s in range(fields):
        for m in range(2):
            for xh in range(2):
                t[s, :, :, m, :, xh, m, s, :] = r.transpose(0, 3, 2, 1)
    return tall(t.reshape(fields * 2 * MX * 2, NX * 2 * 2 * fields * 2))


def x_inverse_table(factor):
    r = rotation(x_places(), signed(MX), NX, 1.0) * factor
    t = np.zeros((NX, 2, 2, 2, 2, 2, MX, 2))
    for s in range(2):
        for m in range(2):
            t[:, m, s, :, s, :, :, m] = r.transpose(2, 0, 1, 3)
    return wide(t.reshape(NX * 8, 128))


def dot(a, b):
    return jnp.dot(a, b, preferred_element_type=F32)


def two(values):
    high = values.astype(BF16)
    return high, (values - high.astype(F32)).astype(BF16)


def three(values):
    high, low = two(values)
    return jnp.concatenate([high, low, high], axis=0)


def tall_dot(table, values):
    rows = table.shape[0] // 2
    high, low = two(values)
    first = dot(table, high)
    return first[:rows] + first[rows:] + dot(table[:rows], low)


def mode_rows(k, extra):
    zh, xh, m = k % 8 // 4, k % 4 // 2, k % 2
    return [pl.ds(zh * 32 + xl * 16 + xh * 8 + m * 4 + extra, 16, stride=64) for xl in range(2)]


def back_rows(k, extra):
    zh, m = k % 4 // 2, k % 2
    return [pl.ds(zh * 16 + xl * 8 + m * 4 + extra, 16, stride=32) for xl in range(2)]


def state_rows_of(k, extra):
    zh, xh, m = k % 8 // 4, k % 4 // 2, k % 2
    return [pl.ds(zh * 16 + xl * 8 + xh * 4 + m * 2 + extra, 16, stride=32) for xl in range(2)]


def rows_forward(values, fields, table, after, y):
    rows = dot(table, jnp.concatenate(two(values), axis=0))
    rows = rows[: 2 * MZ] + rows[2 * MZ :]
    start = pl.multiple_of(y * 2 * MZ, 2 * MZ)
    for s in range(fields):
        after[s, pl.ds(start, 2 * MZ), :] = rows[:, s * C : (s + 1) * C]


def columns_forward(fields, table, after, keep, give):
    pieces = [(k, s) for k in range(MZ) for s in range(fields)]
    for pair in zip(pieces[::2], pieces[1::2]):
        parts = []
        for k, s in pair:
            q = [after[s, pl.ds(2 * k + i, ROWS, stride=2 * MZ), :] for i in range(2)]
            parts.append(jnp.concatenate(q, axis=0))
        rows = dot(table, three(jnp.concatenate(parts, axis=1)))
        for i, (k, s) in enumerate(pair):
            sink = keep if k < 8 else give
            for r in range(2):
                places = mode_rows(k, 2 * s + r) if fields == 2 else state_rows_of(k, r)
                for xl, place in enumerate(places):
                    at = r * MY + xl * 16
                    sink[place, :] = rows[at : at + 16, i * C : (i + 1) * C]


def state_kernel(place, state_, zf_, yf_, keep, give, after, state, zf, yf, arrivals):
    rows_each = ROWS // PIECES
    copies = [pltpu.make_async_copy(zf_.at[place[1]], zf, arrivals.at[0])]
    for i in range(PIECES):
        at = pl.ds(i * rows_each, rows_each)
        copies.append(pltpu.make_async_copy(state_.at[:, at], state.at[:, at], arrivals.at[i + 1]))
    copies.append(pltpu.make_async_copy(yf_.at[place[0]], yf, arrivals.at[PIECES + 1]))
    for copy in copies:
        copy.start()
    copies[0].wait()
    for i in range(PIECES):
        copies[i + 1].wait()
        first = i * rows_each
        planes = jnp.transpose(state[:, first : first + rows_each], (1, 0, 2))
        for y in range(0, rows_each, 2):
            pair = planes[y : y + 2].reshape(2 * C, NZ)
            rows = lax.dot_general(zf[:, :NZ], pair, (((1,), (1,)), ((), ())), preferred_element_type=F32)
            rows = rows[: 2 * MZ] + rows[2 * MZ :]
            for j in range(2):
                after[0, pl.ds((first + y + j) * 2 * MZ, 2 * MZ), :] = rows[:, j * C : (j + 1) * C]
    copies[PIECES + 1].wait()
    columns_forward(1, yf[...], after, keep, give)


def ready_kernel(place, w1_, w2_, yi_, zi_, zf_, yf_, w1, w2, w1t, w2t, yi, zi, zf, yf):
    w1[...] = w1_[...]
    w2[...] = w2_[...]
    w1t[...] = w1_[...].T
    w2t[...] = w2_[...].T
    yi[...] = yi_[0]
    zi[...] = zi_[0]
    zf[...] = zf_[0]
    yf[...] = yf_[0]


def field_kernel(
    q00, q10, q01, q11, state, target, w1, w2, w1t, w2t, yi, zi, zf, yf, keep, give, half, after
):
    step = pl.program_id(0)

    @pl.when(step == 0)
    def _():
        for k in range(MZ):
            source = (q00, q10, q01, q11)[k // 4]
            parts = []
            for s in range(2):
                p = [source[place, :] for i in range(2) for place in back_rows(k, 2 * s + i)]
                parts.append(jnp.concatenate(p, axis=0))
            rows = dot(yi[...], three(jnp.concatenate(parts, axis=1)))
            for s in range(2):
                half[s, pl.ds(k * 64, 64), :] = rows[:, s * C : (s + 1) * C]

    first = step * ROWS_A_STEP
    fields = []
    for i in range(ROWS_A_STEP):
        taken = [half[s, pl.ds(first + i, 2 * MZ, stride=ROWS), :] for s in range(2)]
        fields.append(dot(zi[...], three(jnp.concatenate(taken, axis=1))))
    fields = jnp.concatenate(fields, axis=0).astype(BF16)
    primal, tangent = fields[:, :C], fields[:, C:]
    layer_input = state[...].astype(F32) + primal.astype(F32)
    hidden = dot(layer_input.astype(BF16), w1[...])
    mass = 0.5 * (1.0 + lax.erf(hidden * math.sqrt(0.5)))
    density = jnp.exp(-0.5 * hidden * hidden) * (1.0 / math.sqrt(2.0 * math.pi))
    slope = mass + hidden * density
    activation = (hidden * mass).astype(BF16)
    seed_primal = LOSS_SCALE * (layer_input + dot(activation, w2[...]) - target[...].astype(F32))
    hidden_tangent = dot(tangent, w1[...])
    activation_tangent = (slope * hidden_tangent).astype(BF16)
    seed_tangent = LOSS_SCALE * (tangent.astype(F32) + dot(activation_tangent, w2[...]))
    back_primal = dot(seed_primal.astype(BF16), w2t[...])
    back_tangent = dot(seed_tangent.astype(BF16), w2t[...])
    delta_primal = (slope * back_primal).astype(BF16)
    bend = density * (2.0 - hidden * hidden)
    delta_tangent = (bend * hidden_tangent * back_primal + slope * back_tangent).astype(BF16)
    cotangents = [seed_primal + dot(delta_primal, w1t[...]), seed_tangent + dot(delta_tangent, w1t[...])]
    cotangents = jnp.concatenate(cotangents, axis=1)
    for i in range(ROWS_A_STEP):
        rows_forward(cotangents[i * NZ : (i + 1) * NZ], 2, zf[...], after, first + i)

    @pl.when(step == ROWS // ROWS_A_STEP - 1)
    def _():
        columns_forward(2, yf[...], after, keep, give)


def whole(shape):
    return pl.BlockSpec(shape, lambda i: (0,) * len(shape))


def still(shape):
    return pl.BlockSpec(shape, lambda i, place: (0,) * len(shape))


def picked(table, index):
    return pl.BlockSpec((1,) + table.shape[1:], lambda i, place: (place[index], 0, 0))


FAR = pl.BlockSpec(memory_space=pltpu.HBM)
MIB = 1024 * 1024


def cost(flops, size):
    return pl.CostEstimate(flops=flops, bytes_accessed=size, transcendentals=0)


def stay(array):
    return pltpu.with_memory_space_constraint(array, pltpu.HBM)


def state_stage(place, state, zf, yf):
    shape = jax.ShapeDtypeStruct((512, C), F32)
    return pl.pallas_call(
        state_kernel,
        grid_spec=pltpu.PrefetchScalarGridSpec(
            num_scalar_prefetch=1,
            grid=(1,),
            in_specs=[FAR] * 3,
            out_specs=(still((512, C)), still((512, C))),
            scratch_shapes=[
                pltpu.VMEM((1, 1024, C), F32),
                pltpu.VMEM(state.shape, BF16),
                pltpu.VMEM(zf.shape[1:], BF16),
                pltpu.VMEM(yf.shape[1:], BF16),
                pltpu.SemaphoreType.DMA((PIECES + 2,)),
            ],
        ),
        out_shape=(shape, shape),
        cost_estimate=cost(200_000_000, 8 * MIB),
        compiler_params=params(16),
    )(place, stay(state), stay(zf), stay(yf))


def ready_stage(place, w1, w2, tables):
    shapes = [(C, FF), (FF, C), (FF, C), (C, FF)] + [t.shape[1:] for t in tables]
    return pl.pallas_call(
        ready_kernel,
        grid_spec=pltpu.PrefetchScalarGridSpec(
            num_scalar_prefetch=1,
            grid=(1,),
            in_specs=[still(w1.shape), still(w2.shape)] + [picked(t, i) for t, i in zip(tables, (0, 0, 1, 0))],
            out_specs=tuple(still(shape) for shape in shapes),
        ),
        out_shape=tuple(jax.ShapeDtypeStruct(shape, BF16) for shape in shapes),
        cost_estimate=cost(0, 2 * MIB),
        compiler_params=params(16),
    )(place, w1, w2, *tables)


def field_stage(quarters, state, target, ready):
    moving = pl.BlockSpec((CHUNK, C), lambda i: (i, 0))
    shape = jax.ShapeDtypeStruct((1024, C), F32)
    return pl.pallas_call(
        field_kernel,
        grid=(ROWS // ROWS_A_STEP,),
        in_specs=[whole((512, C))] * 4 + [moving] * 2 + [whole(r.shape) for r in ready],
        out_specs=(whole((1024, C)), whole((1024, C))),
        out_shape=(shape, shape),
        scratch_shapes=[pltpu.VMEM((2, 1024, C), F32), pltpu.VMEM((2, 1024, C), F32)],
        cost_estimate=cost(5_000_000_000, 50 * MIB),
        compiler_params=params(),
    )(*quarters, state, target, *ready)


def mix_kernel(received, weight, direction, xf, xi_, spectra, planes, total, held, xi, arrivals):
    step = pl.program_id(0)
    copies = [
        pltpu.make_async_copy(direction.at[:, pl.ds(i * CB, CB)], held.at[:, pl.ds(i * CB, CB)], arrivals.at[i])
        for i in range(C // CB)
    ]
    last = pltpu.make_async_copy(xi_, xi, arrivals.at[C // CB])

    @pl.when(step == 0)
    def _():
        for copy in copies:
            copy.start()
        last.start()
        spectra[...] = tall_dot(xf[...], received[...])
        total[...] = jnp.zeros_like(total)

    turned = pltpu.roll(spectra[...], C - step * CB, 1)

    def gather(s, pair):
        real_sum, imag_sum = total[2 * s], total[2 * s + 1]
        for j in range(CB):
            column = jnp.broadcast_to(turned[:, j : j + 1], (64, C))
            real, imag = column[:32], column[32:]
            wr, wi = pair(j)
            real_sum = real_sum + (wr * real - wi * imag)
            imag_sum = imag_sum + (wr * imag + wi * real)
        total[2 * s], total[2 * s + 1] = real_sum, imag_sum

    gather(0, lambda j: (weight[0, j].astype(F32), weight[1, j].astype(F32)))
    for i in range(C // CB):

        @pl.when(step == i)
        def _():
            copies[i].wait()

    gather(1, lambda j: (held[0, step * CB + j].astype(F32), held[1, step * CB + j].astype(F32)))

    @pl.when(step == C // CB - 1)
    def _():
        last.wait()
        planes[...] = dot(xi[...], three(total[...].reshape(128, C)))


def mix_stage(received, weight, direction):
    xf = x_forward_table(1, FORWARD_FACTOR)
    xi = x_inverse_table(INVERSE_FACTOR)
    moving = pl.BlockSpec((2, CB, 32, C), lambda i: (0, i, 0, 0))
    return pl.pallas_call(
        mix_kernel,
        grid=(C // CB,),
        in_specs=[whole(received.shape), moving, FAR, whole(xf.shape), FAR],
        out_specs=(whole((64, C)), whole((NX * 8, C))),
        out_shape=(jax.ShapeDtypeStruct((64, C), F32), jax.ShapeDtypeStruct((NX * 8, C), F32)),
        scratch_shapes=[
            pltpu.VMEM((4, 32, C), F32),
            pltpu.VMEM((2, C, 32, C), BF16),
            pltpu.VMEM(xi.shape, BF16),
            pltpu.SemaphoreType.DMA((C // CB + 1,)),
        ],
        cost_estimate=cost(100_000_000, 9 * MIB),
        compiler_params=params(16),
    )(
        received,
        weight.reshape(2, C, 32, C),
        stay(direction.reshape(2, C, 32, C)),
        jnp.asarray(xf),
        stay(jnp.asarray(xi)),
    )


def outer_kernel(received, spectra, xf, gradient, curvature, adjoint):
    step = pl.program_id(0)

    @pl.when(step == 0)
    def _():
        adjoint[...] = tall_dot(xf[...], received[...])

    turned = pltpu.roll(spectra[...], C - step * CB, 1)
    pieces = [adjoint[32 * i : 32 * i + 32, :] for i in range(4)]
    for j in range(CB):
        column = jnp.broadcast_to(turned[:, j : j + 1], (64, C))
        real, imag = column[:32], column[32:]
        for s, sink in ((0, gradient), (1, curvature)):
            re, im = pieces[2 * s], pieces[2 * s + 1]
            sink[0, j] = (real * re + imag * im).astype(BF16)
            sink[1, j] = (real * im - imag * re).astype(BF16)


def outer_stage(received, spectra):
    xf = x_forward_table(2, INVERSE_FACTOR)
    moving = pl.BlockSpec((2, CB, 32, C), lambda i: (0, i, 0, 0))
    shape = jax.ShapeDtypeStruct((2, C, 32, C), BF16)
    return pl.pallas_call(
        outer_kernel,
        grid=(C // CB,),
        in_specs=[whole(received.shape), whole(spectra.shape), whole(xf.shape)],
        out_specs=(moving, moving),
        out_shape=(shape, shape),
        scratch_shapes=[pltpu.VMEM((128, C), F32)],
        cost_estimate=cost(200_000_000, 11 * MIB),
        compiler_params=params(24),
    )(received, spectra, jnp.asarray(xf))


def exchange(rows, group):
    size = lax.axis_size(group)
    return lax.all_to_all(rows.reshape(size, -1, C), group, 0, 0, tiled=True).reshape(rows.shape)


def swap(rows, axis):
    return lax.ppermute(rows, axis, [(0, 1), (1, 0)])


def local(state, target, spectral_weight, direction_weight, inner_weight, outer_weight):
    place = jnp.stack([lax.axis_index(COL), lax.axis_index("co")]).astype(jnp.int32)
    yi, yf = (jnp.asarray(t) for t in y_tables())
    zi, zf = (jnp.asarray(t) for t in z_tables())

    def rows_of(cells):
        return cells[:, 0].transpose(1, 2, 0).reshape(ROWS * NZ, C)

    keep, give = state_stage(place, state.reshape(C, ROWS, NZ), zf, yf)
    received = exchange(keep + swap(give, "co"), WIDE)
    spectra, planes = mix_stage(received, spectral_weight, direction_weight)
    q00 = exchange(planes, WIDE[:3])
    q10 = swap(q00, "xh")
    q01 = swap(q00, "co")
    q00, state, target, w1, w2 = lax.optimization_barrier((q00, state, target, inner_weight, outer_weight))
    ready = ready_stage(place, w1, w2, (yi, zi, zf, yf))
    rows = rows_of(state), rows_of(target)
    q10, ready, rows = lax.optimization_barrier((q10, ready, rows))
    q11 = swap(q10, "co")
    keep, give = field_stage((q00, q10, q01, q11), *rows, ready)
    adjoint = exchange(keep + swap(give, "co"), WIDE)
    gradient, curvature = outer_stage(adjoint, spectra)
    shape = (2, C, MX, 2, C)
    return gradient.reshape(shape), curvature.reshape(shape)


def solution(mesh):
    fine = Mesh(mesh.devices.reshape(2, 4, 8, 2, 2), GX + COL)
    grid = P(None, GX, COL, None)
    blocks = P(None, None, None, GX + COL, None)
    return jax.shard_map(
        local,
        mesh=fine,
        in_specs=(grid, grid, blocks, blocks, P(), P()),
        out_specs=(blocks, blocks),
        check_vma=False,
    )
```

```python
import math

import jax
import jax.numpy as jnp
import ml_dtypes
import numpy as np
from jax import lax
from jax.experimental import pallas as pl
from jax.experimental.pallas import tpu as pltpu
from jax.sharding import Mesh
from jax.sharding import PartitionSpec as P

C = 128
FF = 512
NX = 64
NY = 128
NZ = 128
MX = 16
MY = 32
MZ = 16
ROWS = 32
COLUMNS = 4
POINTS = NX * NY * NZ
KEPT = MX * MY * MZ
FORWARD_FACTOR = 1.0 / math.sqrt(POINTS)
INVERSE_FACTOR = 2.0 / math.sqrt(KEPT)
LOSS_SCALE = 0.5 * math.sqrt(KEPT / POINTS)
ROWS_A_STEP = 16
CHUNK = ROWS_A_STEP * NZ
CB = 64

GX = ("xl", "y", "z")
COL = ("xh", "co")
WIDE = ("y", "z", "xl", "xh")
F32 = jnp.float32
BF16 = jnp.bfloat16


def params(mebibytes=44):
    return pltpu.CompilerParams(dimension_semantics=("arbitrary",), vmem_limit_bytes=mebibytes * 1024 * 1024)


def signed(number):
    ladder = np.arange(number)
    return np.where(ladder < number // 2, ladder, ladder - number)


def angles(positions, frequencies, length):
    return (np.outer(positions, frequencies) % length) * (2.0 * math.pi / length)


def halves(table):
    high = table.astype(ml_dtypes.bfloat16)
    low = (table - high.astype(np.float64)).astype(ml_dtypes.bfloat16)
    return high, low


def wide(table):
    high, low = halves(table)
    return np.concatenate([high, high, low], axis=-1)


def tall(table):
    high, low = halves(table)
    return np.concatenate([high, low], axis=-2)


def rotation(positions, frequencies, length, sign):
    a = angles(positions, frequencies, length)
    c, s = np.cos(a), sign * np.sin(a)
    return np.stack([np.stack([c, -s]), np.stack([s, c])])


def back_order(column):
    order = []
    for part in range(4):
        xh, co = column // 2 ^ part % 2, column % 2 ^ part // 2
        order += [8 * zh + 4 * xh + 2 * co + m for zh in range(2) for m in range(2)]
    return np.array(order)


def out_order(core):
    order = []
    for part in range(2):
        for zh in range(2):
            for xh in range(2):
                order += [8 * zh + 4 * xh + 2 * (core ^ part) + m for m in range(2)]
    return np.array(order)


def z_tables():
    inverse, forward = [], []
    for column in range(COLUMNS):
        a = angles(np.arange(NZ), back_order(column), NZ)
        inverse.append(wide(np.stack([np.cos(a), -np.sin(a)], -1).reshape(NZ, 2 * MZ)))
    for core in range(2):
        a = angles(np.arange(NZ), out_order(core), NZ)
        high, low = halves(np.stack([np.cos(a), -np.sin(a)], -1).reshape(NZ, 2 * MZ).T)
        forward.append(np.block([[high, high], [low, np.zeros_like(low)]]))
    return np.stack(inverse), np.stack(forward)


def y_tables():
    inverse, forward = [], []
    for column in range(COLUMNS):
        rows = column * ROWS + np.arange(ROWS)
        r = rotation(rows, signed(MY), NY, 1.0)
        inverse.append(wide(r.transpose(0, 2, 1, 3).reshape(2 * ROWS, 2 * MY)))
        r = rotation(rows, signed(MY), NY, -1.0)
        forward.append(wide(r.transpose(0, 3, 1, 2).reshape(2 * MY, 2 * ROWS)))
    return np.stack(inverse), np.stack(forward)


def x_places():
    return np.arange(NX).reshape(2, 4, 8).transpose(1, 2, 0).reshape(NX)


def x_forward_table(fields, factor):
    r = rotation(x_places(), signed(MX), NX, -1.0) * factor
    t = np.zeros((fields, 2, MX, 2, NX, 2, 2, fields, 2))
    for s in range(fields):
        for m in range(2):
            for xh in range(2):
                t[s, :, :, m, :, xh, m, s, :] = r.transpose(0, 3, 2, 1)
    return tall(t.reshape(fields * 2 * MX * 2, NX * 2 * 2 * fields * 2))


def x_inverse_table(factor):
    r = rotation(x_places(), signed(MX), NX, 1.0) * factor
    t = np.zeros((NX, 2, 2, 2, 2, 2, MX, 2))
    for s in range(2):
        for m in range(2):
            t[:, m, s, :, s, :, :, m] = r.transpose(2, 0, 1, 3)
    return wide(t.reshape(NX * 8, 128))


def dot(a, b):
    return jnp.dot(a, b, preferred_element_type=F32)


def two(values):
    high = values.astype(BF16)
    return high, (values - high.astype(F32)).astype(BF16)


def three(values):
    high, low = two(values)
    return jnp.concatenate([high, low, high], axis=0)


def tall_dot(table, values):
    rows = table.shape[0] // 2
    high, low = two(values)
    first = dot(table, high)
    return first[:rows] + first[rows:] + dot(table[:rows], low)


def mode_rows(k, extra):
    zh, xh, m = k % 8 // 4, k % 4 // 2, k % 2
    return [pl.ds(zh * 32 + xl * 16 + xh * 8 + m * 4 + extra, 16, stride=64) for xl in range(2)]


def back_rows(k, extra):
    zh, m = k % 4 // 2, k % 2
    return [pl.ds(zh * 16 + xl * 8 + m * 4 + extra, 16, stride=32) for xl in range(2)]


def state_rows_of(k, extra):
    zh, xh, m = k % 8 // 4, k % 4 // 2, k % 2
    return [pl.ds(zh * 16 + xl * 8 + xh * 4 + m * 2 + extra, 16, stride=32) for xl in range(2)]


def rows_forward(values, fields, table, after, y):
    rows = dot(table, jnp.concatenate(two(values), axis=0))
    rows = rows[: 2 * MZ] + rows[2 * MZ :]
    start = pl.multiple_of(y * 2 * MZ, 2 * MZ)
    for s in range(fields):
        after[s, pl.ds(start, 2 * MZ), :] = rows[:, s * C : (s + 1) * C]


def columns_forward(fields, table, after, keep, give):
    pieces = [(k, s) for k in range(MZ) for s in range(fields)]
    for pair in zip(pieces[::2], pieces[1::2]):
        parts = []
        for k, s in pair:
            q = [after[s, pl.ds(2 * k + i, ROWS, stride=2 * MZ), :] for i in range(2)]
            parts.append(jnp.concatenate(q, axis=0))
        rows = dot(table, three(jnp.concatenate(parts, axis=1)))
        for i, (k, s) in enumerate(pair):
            sink = keep if k < 8 else give
            for r in range(2):
                places = mode_rows(k, 2 * s + r) if fields == 2 else state_rows_of(k, r)
                for xl, place in enumerate(places):
                    at = r * MY + xl * 16
                    sink[place, :] = rows[at : at + 16, i * C : (i + 1) * C]


def state_kernel(place, state, zf, yf, keep, give, after):
    for y in range(0, ROWS, 2):
        pair = jnp.concatenate([state[(y + i) * NZ : (y + i + 1) * NZ] for i in range(2)], axis=1)
        rows = dot(zf[0, :, :NZ], pair)
        rows = rows[: 2 * MZ] + rows[2 * MZ :]
        for i in range(2):
            after[0, pl.ds((y + i) * 2 * MZ, 2 * MZ), :] = rows[:, i * C : (i + 1) * C]
    columns_forward(1, yf[0], after, keep, give)


def ready_kernel(place, w1_, w2_, yi_, zi_, zf_, yf_, w1, w2, w1t, w2t, yi, zi, zf, yf):
    w1[...] = w1_[...]
    w2[...] = w2_[...]
    w1t[...] = w1_[...].T
    w2t[...] = w2_[...].T
    yi[...] = yi_[0]
    zi[...] = zi_[0]
    zf[...] = zf_[0]
    yf[...] = yf_[0]


def y_inverse(parts, table, half):
    for k in range(4 * len(parts)):
        rows = []
        for s in range(2):
            p = [parts[k // 4][place, :] for i in range(2) for place in back_rows(k, 2 * s + i)]
            rows.append(jnp.concatenate(p, axis=0))
        rows = dot(table, three(jnp.concatenate(rows, axis=1)))
        for s in range(2):
            half[s, pl.ds(k * 64, 64), :] = rows[:, s * C : (s + 1) * C]


def early_kernel(q00, q10, q01, yi, half):
    y_inverse((q00, q10, q01), yi[...], half)


def field_kernel(
    early, q11, state, target, w1, w2, w1t, w2t, yi, zi, zf, yf, keep, give, late, after
):
    step = pl.program_id(0)

    @pl.when(step == 0)
    def _():
        y_inverse((q11,), yi[...], late)

    first = step * ROWS_A_STEP
    fields = []
    for i in range(ROWS_A_STEP):
        taken = []
        for part, count in ((early, 24), (late, 8)):
            taken.append(jnp.concatenate([part[s, pl.ds(first + i, count, stride=ROWS), :] for s in range(2)], axis=1))
        fields.append(dot(zi[...], three(jnp.concatenate(taken, axis=0))))
    fields = jnp.concatenate(fields, axis=0).astype(BF16)
    primal, tangent = fields[:, :C], fields[:, C:]
    layer_input = state[...].astype(F32) + primal.astype(F32)
    hidden = dot(layer_input.astype(BF16), w1[...])
    mass = 0.5 * (1.0 + lax.erf(hidden * math.sqrt(0.5)))
    density = jnp.exp(-0.5 * hidden * hidden) * (1.0 / math.sqrt(2.0 * math.pi))
    slope = mass + hidden * density
    activation = (hidden * mass).astype(BF16)
    seed_primal = LOSS_SCALE * (layer_input + dot(activation, w2[...]) - target[...].astype(F32))
    hidden_tangent = dot(tangent, w1[...])
    activation_tangent = (slope * hidden_tangent).astype(BF16)
    seed_tangent = LOSS_SCALE * (tangent.astype(F32) + dot(activation_tangent, w2[...]))
    back_primal = dot(seed_primal.astype(BF16), w2t[...])
    back_tangent = dot(seed_tangent.astype(BF16), w2t[...])
    delta_primal = (slope * back_primal).astype(BF16)
    bend = density * (2.0 - hidden * hidden)
    delta_tangent = (bend * hidden_tangent * back_primal + slope * back_tangent).astype(BF16)
    cotangents = [seed_primal + dot(delta_primal, w1t[...]), seed_tangent + dot(delta_tangent, w1t[...])]
    cotangents = jnp.concatenate(cotangents, axis=1)
    for i in range(ROWS_A_STEP):
        rows_forward(cotangents[i * NZ : (i + 1) * NZ], 2, zf[...], after, first + i)

    @pl.when(step == ROWS // ROWS_A_STEP - 1)
    def _():
        columns_forward(2, yf[...], after, keep, give)


def whole(shape):
    return pl.BlockSpec(shape, lambda i: (0,) * len(shape))


def still(shape):
    return pl.BlockSpec(shape, lambda i, place: (0,) * len(shape))


def picked(table, index):
    return pl.BlockSpec((1,) + table.shape[1:], lambda i, place: (place[index], 0, 0))


def state_stage(place, state, zf, yf):
    shape = jax.ShapeDtypeStruct((512, C), F32)
    return pl.pallas_call(
        state_kernel,
        grid_spec=pltpu.PrefetchScalarGridSpec(
            num_scalar_prefetch=1,
            grid=(1,),
            in_specs=[still(state.shape), picked(zf, 1), picked(yf, 0)],
            out_specs=(still((512, C)), still((512, C))),
            scratch_shapes=[pltpu.VMEM((1, 1024, C), F32)],
        ),
        out_shape=(shape, shape),
        compiler_params=params(),
    )(place, state, zf, yf)


def ready_stage(place, w1, w2, tables):
    shapes = [(C, FF), (FF, C), (FF, C), (C, FF)] + [t.shape[1:] for t in tables]
    return pl.pallas_call(
        ready_kernel,
        grid_spec=pltpu.PrefetchScalarGridSpec(
            num_scalar_prefetch=1,
            grid=(1,),
            in_specs=[still(w1.shape), still(w2.shape)] + [picked(t, i) for t, i in zip(tables, (0, 0, 1, 0))],
            out_specs=tuple(still(shape) for shape in shapes),
        ),
        out_shape=tuple(jax.ShapeDtypeStruct(shape, BF16) for shape in shapes),
        compiler_params=params(16),
    )(place, w1, w2, *tables)


def early_stage(q00, q10, q01, yi):
    shape = (2, 768, C)
    return pl.pallas_call(
        early_kernel,
        grid=(1,),
        in_specs=[whole((512, C))] * 3 + [whole(yi.shape)],
        out_specs=whole(shape),
        out_shape=jax.ShapeDtypeStruct(shape, F32),
        compiler_params=params(16),
    )(q00, q10, q01, yi)


def field_stage(early, q11, state, target, ready):
    moving = pl.BlockSpec((CHUNK, C), lambda i: (i, 0))
    shape = jax.ShapeDtypeStruct((1024, C), F32)
    return pl.pallas_call(
        field_kernel,
        grid=(ROWS // ROWS_A_STEP,),
        in_specs=[whole(early.shape), whole((512, C))] + [moving] * 2 + [whole(r.shape) for r in ready],
        out_specs=(whole((1024, C)), whole((1024, C))),
        out_shape=(shape, shape),
        scratch_shapes=[pltpu.VMEM((2, 256, C), F32), pltpu.VMEM((2, 1024, C), F32)],
        compiler_params=params(),
    )(early, q11, state, target, *ready)


def mix_kernel(received, weight, direction, xf, xi_, spectra, planes, total, xi, arrival):
    step = pl.program_id(0)
    second = pltpu.make_async_copy(xi_, xi, arrival)

    @pl.when(step == 0)
    def _():
        second.start()
        spectra[...] = tall_dot(xf[...], received[...])
        total[...] = jnp.zeros_like(total)

    turned = pltpu.roll(spectra[...], C - step * CB, 1)
    sums = [total[i] for i in range(4)]
    for j in range(CB):
        column = jnp.broadcast_to(turned[:, j : j + 1], (64, C))
        real, imag = column[:32], column[32:]
        for s, w in ((0, weight), (1, direction)):
            wr, wi = w[0, j].astype(F32), w[1, j].astype(F32)
            sums[2 * s] = sums[2 * s] + (wr * real - wi * imag)
            sums[2 * s + 1] = sums[2 * s + 1] + (wr * imag + wi * real)
    for i in range(4):
        total[i] = sums[i]

    @pl.when(step == C // CB - 1)
    def _():
        second.wait()
        out = dot(xi[...], three(jnp.concatenate(sums, axis=0)))
        planes[...] = out


def mix_stage(received, weight, direction):
    xf = x_forward_table(1, FORWARD_FACTOR)
    xi = x_inverse_table(INVERSE_FACTOR)
    weight = weight.reshape(2, C, 32, C)
    direction = direction.reshape(2, C, 32, C)
    moving = pl.BlockSpec((2, CB, 32, C), lambda i: (0, i, 0, 0))
    return pl.pallas_call(
        mix_kernel,
        grid=(C // CB,),
        in_specs=[whole(received.shape), moving, moving, whole(xf.shape), pl.BlockSpec(memory_space=pltpu.HBM)],
        out_specs=(whole((64, C)), whole((NX * 8, C))),
        out_shape=(jax.ShapeDtypeStruct((64, C), F32), jax.ShapeDtypeStruct((NX * 8, C), F32)),
        scratch_shapes=[
            pltpu.VMEM((4, 32, C), F32),
            pltpu.VMEM(xi.shape, BF16),
            pltpu.SemaphoreType.DMA,
        ],
        compiler_params=params(),
    )(received, weight, direction, jnp.asarray(xf), pltpu.with_memory_space_constraint(jnp.asarray(xi), pltpu.HBM))


def outer_kernel(received, spectra, xf, gradient, curvature, adjoint):
    step = pl.program_id(0)

    @pl.when(step == 0)
    def _():
        adjoint[...] = tall_dot(xf[...], received[...])

    turned = pltpu.roll(spectra[...], C - step * CB, 1)
    pieces = [adjoint[32 * i : 32 * i + 32, :] for i in range(4)]
    for j in range(CB):
        column = jnp.broadcast_to(turned[:, j : j + 1], (64, C))
        real, imag = column[:32], column[32:]
        for s, sink in ((0, gradient), (1, curvature)):
            re, im = pieces[2 * s], pieces[2 * s + 1]
            sink[0, j] = (real * re + imag * im).astype(BF16)
            sink[1, j] = (real * im - imag * re).astype(BF16)


def outer_stage(received, spectra):
    xf = x_forward_table(2, INVERSE_FACTOR)
    moving = pl.BlockSpec((2, CB, 32, C), lambda i: (0, i, 0, 0))
    shape = jax.ShapeDtypeStruct((2, C, 32, C), BF16)
    return pl.pallas_call(
        outer_kernel,
        grid=(C // CB,),
        in_specs=[whole(received.shape), whole(spectra.shape), whole(xf.shape)],
        out_specs=(moving, moving),
        out_shape=(shape, shape),
        scratch_shapes=[pltpu.VMEM((128, C), F32)],
        compiler_params=params(),
    )(received, spectra, jnp.asarray(xf))


def exchange(rows, group):
    size = lax.axis_size(group)
    return lax.all_to_all(rows.reshape(size, -1, C), group, 0, 0, tiled=True).reshape(rows.shape)


def swap(rows, axis):
    return lax.ppermute(rows, axis, [(0, 1), (1, 0)])


def local(state, target, spectral_weight, direction_weight, inner_weight, outer_weight):
    place = jnp.stack([lax.axis_index(COL), lax.axis_index("co")]).astype(jnp.int32)
    yi, yf = (jnp.asarray(t) for t in y_tables())
    zi, zf = (jnp.asarray(t) for t in z_tables())

    def rows_of(cells):
        return cells[:, 0].transpose(1, 2, 0).reshape(ROWS * NZ, C)

    state_rows = rows_of(state)
    keep, give = state_stage(place, state_rows, zf, yf)
    received = exchange(keep + swap(give, "co"), WIDE)
    spectra, planes = mix_stage(received, spectral_weight, direction_weight)
    q00 = exchange(planes, WIDE[:3])
    q10 = swap(q00, "xh")
    q01 = swap(q00, "co")
    q00, target, w1, w2 = lax.optimization_barrier((q00, target, inner_weight, outer_weight))
    ready = ready_stage(place, w1, w2, (yi, zi, zf, yf))
    target_rows = rows_of(target)
    q10, ready, target_rows = lax.optimization_barrier((q10, ready, target_rows))
    q11 = swap(q10, "co")
    early = early_stage(q00, q10, q01, ready[4])
    keep, give = field_stage(early, q11, state_rows, target_rows, ready)
    adjoint = exchange(keep + swap(give, "co"), WIDE)
    gradient, curvature = outer_stage(adjoint, spectra)
    shape = (2, C, MX, 2, C)
    return gradient.reshape(shape), curvature.reshape(shape)


def solution(mesh):
    fine = Mesh(mesh.devices.reshape(2, 4, 8, 2, 2), GX + COL)
    grid = P(None, GX, COL, None)
    blocks = P(None, None, None, GX + COL, None)
    return jax.shard_map(
        local,
        mesh=fine,
        in_specs=(grid, grid, blocks, blocks, P(), P()),
        out_specs=(blocks, blocks),
        check_vma=False,
    )
```

```python
import math

import jax
import jax.numpy as jnp
import ml_dtypes
import numpy as np
from jax import lax
from jax.experimental import pallas as pl
from jax.experimental.pallas import tpu as pltpu
from jax.sharding import Mesh
from jax.sharding import PartitionSpec as P

C = 128
FF = 512
NX = 64
NY = 128
NZ = 128
MX = 16
MY = 32
MZ = 16
ROWS = 32
COLUMNS = 4
POINTS = NX * NY * NZ
KEPT = MX * MY * MZ
FORWARD_FACTOR = 1.0 / math.sqrt(POINTS)
INVERSE_FACTOR = 2.0 / math.sqrt(KEPT)
LOSS_SCALE = 0.5 * math.sqrt(KEPT / POINTS)
ROWS_A_STEP = 16
CHUNK = ROWS_A_STEP * NZ
CB = 64

GX = ("xl", "y", "z")
COL = ("xh", "co")
WIDE = ("y", "z", "xl", "xh")
F32 = jnp.float32
BF16 = jnp.bfloat16


def params(mebibytes=44):
    return pltpu.CompilerParams(dimension_semantics=("arbitrary",), vmem_limit_bytes=mebibytes * 1024 * 1024)


def signed(number):
    ladder = np.arange(number)
    return np.where(ladder < number // 2, ladder, ladder - number)


def angles(positions, frequencies, length):
    return (np.outer(positions, frequencies) % length) * (2.0 * math.pi / length)


def halves(table):
    high = table.astype(ml_dtypes.bfloat16)
    low = (table - high.astype(np.float64)).astype(ml_dtypes.bfloat16)
    return high, low


def wide(table):
    high, low = halves(table)
    return np.concatenate([high, high, low], axis=-1)


def tall(table):
    high, low = halves(table)
    return np.concatenate([high, low], axis=-2)


def rotation(positions, frequencies, length, sign):
    a = angles(positions, frequencies, length)
    c, s = np.cos(a), sign * np.sin(a)
    return np.stack([np.stack([c, -s]), np.stack([s, c])])


def back_order(column):
    order = []
    for part in range(4):
        xh, co = column // 2 ^ part % 2, column % 2 ^ part // 2
        order += [8 * zh + 4 * xh + 2 * co + m for zh in range(2) for m in range(2)]
    return np.array(order)


def out_order(core):
    order = []
    for part in range(2):
        for zh in range(2):
            for xh in range(2):
                order += [8 * zh + 4 * xh + 2 * (core ^ part) + m for m in range(2)]
    return np.array(order)


def z_tables():
    inverse, forward = [], []
    for column in range(COLUMNS):
        a = angles(np.arange(NZ), back_order(column), NZ)
        inverse.append(wide(np.stack([np.cos(a), -np.sin(a)], -1).reshape(NZ, 2 * MZ)))
    for core in range(2):
        a = angles(np.arange(NZ), out_order(core), NZ)
        high, low = halves(np.stack([np.cos(a), -np.sin(a)], -1).reshape(NZ, 2 * MZ).T)
        forward.append(np.block([[high, high], [low, np.zeros_like(low)]]))
    return np.stack(inverse), np.stack(forward)


def y_tables():
    inverse, forward = [], []
    for column in range(COLUMNS):
        rows = column * ROWS + np.arange(ROWS)
        r = rotation(rows, signed(MY), NY, 1.0)
        inverse.append(wide(r.transpose(0, 2, 1, 3).reshape(2 * ROWS, 2 * MY)))
        r = rotation(rows, signed(MY), NY, -1.0)
        forward.append(wide(r.transpose(0, 3, 1, 2).reshape(2 * MY, 2 * ROWS)))
    return np.stack(inverse), np.stack(forward)


def x_places():
    return np.arange(NX).reshape(2, 4, 8).transpose(1, 2, 0).reshape(NX)


def x_forward_table(fields, factor):
    r = rotation(x_places(), signed(MX), NX, -1.0) * factor
    t = np.zeros((fields, 2, MX, 2, NX, 2, 2, fields, 2))
    for s in range(fields):
        for m in range(2):
            for xh in range(2):
                t[s, :, :, m, :, xh, m, s, :] = r.transpose(0, 3, 2, 1)
    return tall(t.reshape(fields * 2 * MX * 2, NX * 2 * 2 * fields * 2))


def x_inverse_table(factor):
    r = rotation(x_places(), signed(MX), NX, 1.0) * factor
    t = np.zeros((NX, 2, 2, 2, 2, 2, MX, 2))
    for s in range(2):
        for m in range(2):
            t[:, m, s, :, s, :, :, m] = r.transpose(2, 0, 1, 3)
    return wide(t.reshape(NX * 8, 128))


def dot(a, b):
    return jnp.dot(a, b, preferred_element_type=F32)


def two(values):
    high = values.astype(BF16)
    return high, (values - high.astype(F32)).astype(BF16)


def three(values):
    high, low = two(values)
    return jnp.concatenate([high, low, high], axis=0)


def tall_dot(table, values):
    rows = table.shape[0] // 2
    high, low = two(values)
    first = dot(table, high)
    return first[:rows] + first[rows:] + dot(table[:rows], low)


def mode_rows(k, extra):
    zh, xh, m = k % 8 // 4, k % 4 // 2, k % 2
    return [pl.ds(zh * 32 + xl * 16 + xh * 8 + m * 4 + extra, 16, stride=64) for xl in range(2)]


def back_rows(k, extra):
    zh, m = k % 4 // 2, k % 2
    return [pl.ds(zh * 16 + xl * 8 + m * 4 + extra, 16, stride=32) for xl in range(2)]


def state_rows_of(k, extra):
    zh, xh, m = k % 8 // 4, k % 4 // 2, k % 2
    return [pl.ds(zh * 16 + xl * 8 + xh * 4 + m * 2 + extra, 16, stride=32) for xl in range(2)]


def rows_forward(values, fields, table, after, y):
    rows = dot(table, jnp.concatenate(two(values), axis=0))
    rows = rows[: 2 * MZ] + rows[2 * MZ :]
    start = pl.multiple_of(y * 2 * MZ, 2 * MZ)
    for s in range(fields):
        after[s, pl.ds(start, 2 * MZ), :] = rows[:, s * C : (s + 1) * C]


def columns_forward(fields, table, after, sink, half):
    pieces = [(k, s) for k in range(8 * half, 8 * half + 8) for s in range(fields)]
    for pair in zip(pieces[::2], pieces[1::2]):
        parts = []
        for k, s in pair:
            q = [after[s, pl.ds(2 * k + i, ROWS, stride=2 * MZ), :] for i in range(2)]
            parts.append(jnp.concatenate(q, axis=0))
        rows = dot(table, three(jnp.concatenate(parts, axis=1)))
        for i, (k, s) in enumerate(pair):
            for r in range(2):
                places = mode_rows(k, 2 * s + r) if fields == 2 else state_rows_of(k, r)
                for xl, place in enumerate(places):
                    at = r * MY + xl * 16
                    sink[place, :] = rows[at : at + 16, i * C : (i + 1) * C]


def kept_kernel(place, after, yf, keep):
    columns_forward(after.shape[0], yf[0], after, keep, 0)


def kept_stage(place, after, yf):
    shape = (512 * after.shape[0], C)
    return pl.pallas_call(
        kept_kernel,
        grid_spec=pltpu.PrefetchScalarGridSpec(
            num_scalar_prefetch=1,
            grid=(1,),
            in_specs=[still(after.shape), picked(yf, 0)],
            out_specs=still(shape),
        ),
        out_shape=jax.ShapeDtypeStruct(shape, F32),
        compiler_params=params(16),
    )(place, after, yf)


def state_kernel(place, state, zf, yf, after, give):
    for y in range(0, ROWS, 2):
        pair = jnp.concatenate([state[(y + i) * NZ : (y + i + 1) * NZ] for i in range(2)], axis=1)
        rows = dot(zf[0, :, :NZ], pair)
        rows = rows[: 2 * MZ] + rows[2 * MZ :]
        for i in range(2):
            after[0, pl.ds((y + i) * 2 * MZ, 2 * MZ), :] = rows[:, i * C : (i + 1) * C]
    columns_forward(1, yf[0], after, give, 1)


def ready_kernel(place, w1_, w2_, yi_, zi_, zf_, yf_, w1, w2, w1t, w2t, yi, zi, zf, yf):
    w1[...] = w1_[...]
    w2[...] = w2_[...]
    w1t[...] = w1_[...].T
    w2t[...] = w2_[...].T
    yi[...] = yi_[0]
    zi[...] = zi_[0]
    zf[...] = zf_[0]
    yf[...] = yf_[0]


def y_inverse(parts, table, half):
    for k in range(4 * len(parts)):
        rows = []
        for s in range(2):
            p = [parts[k // 4][place, :] for i in range(2) for place in back_rows(k, 2 * s + i)]
            rows.append(jnp.concatenate(p, axis=0))
        rows = dot(table, three(jnp.concatenate(rows, axis=1)))
        for s in range(2):
            half[s, pl.ds(k * 64, 64), :] = rows[:, s * C : (s + 1) * C]


def early_kernel(q00, q10, q01, yi, half):
    y_inverse((q00, q10, q01), yi[...], half)


def field_kernel(
    early, q11, state, target, w1, w2, w1t, w2t, yi, zi, zf, yf, after, give, late
):
    step = pl.program_id(0)

    @pl.when(step == 0)
    def _():
        y_inverse((q11,), yi[...], late)

    first = step * ROWS_A_STEP
    fields = []
    for i in range(ROWS_A_STEP):
        taken = []
        for part, count in ((early, 24), (late, 8)):
            taken.append(jnp.concatenate([part[s, pl.ds(first + i, count, stride=ROWS), :] for s in range(2)], axis=1))
        fields.append(dot(zi[...], three(jnp.concatenate(taken, axis=0))))
    fields = jnp.concatenate(fields, axis=0).astype(BF16)
    primal, tangent = fields[:, :C], fields[:, C:]
    layer_input = state[...].astype(F32) + primal.astype(F32)
    hidden = dot(layer_input.astype(BF16), w1[...])
    mass = 0.5 * (1.0 + lax.erf(hidden * math.sqrt(0.5)))
    density = jnp.exp(-0.5 * hidden * hidden) * (1.0 / math.sqrt(2.0 * math.pi))
    slope = mass + hidden * density
    activation = (hidden * mass).astype(BF16)
    seed_primal = LOSS_SCALE * (layer_input + dot(activation, w2[...]) - target[...].astype(F32))
    hidden_tangent = dot(tangent, w1[...])
    activation_tangent = (slope * hidden_tangent).astype(BF16)
    seed_tangent = LOSS_SCALE * (tangent.astype(F32) + dot(activation_tangent, w2[...]))
    back_primal = dot(seed_primal.astype(BF16), w2t[...])
    back_tangent = dot(seed_tangent.astype(BF16), w2t[...])
    delta_primal = (slope * back_primal).astype(BF16)
    bend = density * (2.0 - hidden * hidden)
    delta_tangent = (bend * hidden_tangent * back_primal + slope * back_tangent).astype(BF16)
    cotangents = [seed_primal + dot(delta_primal, w1t[...]), seed_tangent + dot(delta_tangent, w1t[...])]
    cotangents = jnp.concatenate(cotangents, axis=1)
    for i in range(ROWS_A_STEP):
        rows_forward(cotangents[i * NZ : (i + 1) * NZ], 2, zf[...], after, first + i)

    @pl.when(step == ROWS // ROWS_A_STEP - 1)
    def _():
        columns_forward(2, yf[...], after, give, 1)


def whole(shape):
    return pl.BlockSpec(shape, lambda i: (0,) * len(shape))


def still(shape):
    return pl.BlockSpec(shape, lambda i, place: (0,) * len(shape))


def picked(table, index):
    return pl.BlockSpec((1,) + table.shape[1:], lambda i, place: (place[index], 0, 0))


def state_stage(place, state, zf, yf):
    shapes = (1, 1024, C), (512, C)
    return pl.pallas_call(
        state_kernel,
        grid_spec=pltpu.PrefetchScalarGridSpec(
            num_scalar_prefetch=1,
            grid=(1,),
            in_specs=[still(state.shape), picked(zf, 1), picked(yf, 0)],
            out_specs=tuple(still(shape) for shape in shapes),
        ),
        out_shape=tuple(jax.ShapeDtypeStruct(shape, F32) for shape in shapes),
        compiler_params=params(),
    )(place, state, zf, yf)


def ready_stage(place, w1, w2, tables):
    shapes = [(C, FF), (FF, C), (FF, C), (C, FF)] + [t.shape[1:] for t in tables]
    return pl.pallas_call(
        ready_kernel,
        grid_spec=pltpu.PrefetchScalarGridSpec(
            num_scalar_prefetch=1,
            grid=(1,),
            in_specs=[still(w1.shape), still(w2.shape)] + [picked(t, i) for t, i in zip(tables, (0, 0, 1, 0))],
            out_specs=tuple(still(shape) for shape in shapes),
        ),
        out_shape=tuple(jax.ShapeDtypeStruct(shape, BF16) for shape in shapes),
        compiler_params=params(16),
    )(place, w1, w2, *tables)


def early_stage(q00, q10, q01, yi):
    shape = (2, 768, C)
    return pl.pallas_call(
        early_kernel,
        grid=(1,),
        in_specs=[whole((512, C))] * 3 + [whole(yi.shape)],
        out_specs=whole(shape),
        out_shape=jax.ShapeDtypeStruct(shape, F32),
        compiler_params=params(16),
    )(q00, q10, q01, yi)


def field_stage(early, q11, state, target, ready):
    moving = pl.BlockSpec((CHUNK, C), lambda i: (i, 0))
    shapes = (2, 1024, C), (1024, C)
    return pl.pallas_call(
        field_kernel,
        grid=(ROWS // ROWS_A_STEP,),
        in_specs=[whole(early.shape), whole((512, C))] + [moving] * 2 + [whole(r.shape) for r in ready],
        out_specs=tuple(whole(shape) for shape in shapes),
        out_shape=tuple(jax.ShapeDtypeStruct(shape, F32) for shape in shapes),
        scratch_shapes=[pltpu.VMEM((2, 256, C), F32)],
        compiler_params=params(),
    )(early, q11, state, target, *ready)


def mix_kernel(received, weight, direction, xf, xi_, spectra, planes, total, xi, arrival):
    step = pl.program_id(0)
    second = pltpu.make_async_copy(xi_, xi, arrival)

    @pl.when(step == 0)
    def _():
        second.start()
        spectra[...] = tall_dot(xf[...], received[...])
        total[...] = jnp.zeros_like(total)

    turned = pltpu.roll(spectra[...], C - step * CB, 1)
    sums = [total[i] for i in range(4)]
    for j in range(CB):
        column = jnp.broadcast_to(turned[:, j : j + 1], (64, C))
        real, imag = column[:32], column[32:]
        for s, w in ((0, weight), (1, direction)):
            wr, wi = w[0, j].astype(F32), w[1, j].astype(F32)
            sums[2 * s] = sums[2 * s] + (wr * real - wi * imag)
            sums[2 * s + 1] = sums[2 * s + 1] + (wr * imag + wi * real)
    for i in range(4):
        total[i] = sums[i]

    @pl.when(step == C // CB - 1)
    def _():
        second.wait()
        out = dot(xi[...], three(jnp.concatenate(sums, axis=0)))
        planes[...] = out


def mix_stage(received, weight, direction):
    xf = x_forward_table(1, FORWARD_FACTOR)
    xi = x_inverse_table(INVERSE_FACTOR)
    weight = weight.reshape(2, C, 32, C)
    direction = direction.reshape(2, C, 32, C)
    moving = pl.BlockSpec((2, CB, 32, C), lambda i: (0, i, 0, 0))
    return pl.pallas_call(
        mix_kernel,
        grid=(C // CB,),
        in_specs=[whole(received.shape), moving, moving, whole(xf.shape), pl.BlockSpec(memory_space=pltpu.HBM)],
        out_specs=(whole((64, C)), whole((NX * 8, C))),
        out_shape=(jax.ShapeDtypeStruct((64, C), F32), jax.ShapeDtypeStruct((NX * 8, C), F32)),
        scratch_shapes=[
            pltpu.VMEM((4, 32, C), F32),
            pltpu.VMEM(xi.shape, BF16),
            pltpu.SemaphoreType.DMA,
        ],
        compiler_params=params(),
    )(received, weight, direction, jnp.asarray(xf), pltpu.with_memory_space_constraint(jnp.asarray(xi), pltpu.HBM))


def outer_kernel(received, spectra, xf, gradient, curvature, adjoint):
    step = pl.program_id(0)

    @pl.when(step == 0)
    def _():
        adjoint[...] = tall_dot(xf[...], received[...])

    turned = pltpu.roll(spectra[...], C - step * CB, 1)
    pieces = [adjoint[32 * i : 32 * i + 32, :] for i in range(4)]
    for j in range(CB):
        column = jnp.broadcast_to(turned[:, j : j + 1], (64, C))
        real, imag = column[:32], column[32:]
        for s, sink in ((0, gradient), (1, curvature)):
            re, im = pieces[2 * s], pieces[2 * s + 1]
            sink[0, j] = (real * re + imag * im).astype(BF16)
            sink[1, j] = (real * im - imag * re).astype(BF16)


def outer_stage(received, spectra):
    xf = x_forward_table(2, INVERSE_FACTOR)
    moving = pl.BlockSpec((2, CB, 32, C), lambda i: (0, i, 0, 0))
    shape = jax.ShapeDtypeStruct((2, C, 32, C), BF16)
    return pl.pallas_call(
        outer_kernel,
        grid=(C // CB,),
        in_specs=[whole(received.shape), whole(spectra.shape), whole(xf.shape)],
        out_specs=(moving, moving),
        out_shape=(shape, shape),
        scratch_shapes=[pltpu.VMEM((128, C), F32)],
        compiler_params=params(),
    )(received, spectra, jnp.asarray(xf))


def exchange(rows, group):
    size = lax.axis_size(group)
    return lax.all_to_all(rows.reshape(size, -1, C), group, 0, 0, tiled=True).reshape(rows.shape)


def swap(rows, axis):
    return lax.ppermute(rows, axis, [(0, 1), (1, 0)])


def local(state, target, spectral_weight, direction_weight, inner_weight, outer_weight):
    place = jnp.stack([lax.axis_index(COL), lax.axis_index("co")]).astype(jnp.int32)
    yi, yf = (jnp.asarray(t) for t in y_tables())
    zi, zf = (jnp.asarray(t) for t in z_tables())

    def rows_of(cells):
        return cells[:, 0].transpose(1, 2, 0).reshape(ROWS * NZ, C)

    state_rows = rows_of(state)
    after, give = state_stage(place, state_rows, zf, yf)
    received = exchange(swap(give, "co") + kept_stage(place, after, yf), WIDE)
    spectra, planes = mix_stage(received, spectral_weight, direction_weight)
    q00 = exchange(planes, WIDE[:3])
    q10 = swap(q00, "xh")
    q01 = swap(q00, "co")
    q00, target, w1, w2 = lax.optimization_barrier((q00, target, inner_weight, outer_weight))
    ready = ready_stage(place, w1, w2, (yi, zi, zf, yf))
    target_rows = rows_of(target)
    q10, ready, target_rows = lax.optimization_barrier((q10, ready, target_rows))
    q11 = swap(q10, "co")
    early = early_stage(q00, q10, q01, ready[4])
    after, give = field_stage(early, q11, state_rows, target_rows, ready)
    adjoint = exchange(swap(give, "co") + kept_stage(0 * place, after, ready[7][None]), WIDE)
    gradient, curvature = outer_stage(adjoint, spectra)
    shape = (2, C, MX, 2, C)
    return gradient.reshape(shape), curvature.reshape(shape)


def solution(mesh):
    fine = Mesh(mesh.devices.reshape(2, 4, 8, 2, 2), GX + COL)
    grid = P(None, GX, COL, None)
    blocks = P(None, None, None, GX + COL, None)
    return jax.shard_map(
        local,
        mesh=fine,
        in_specs=(grid, grid, blocks, blocks, P(), P()),
        out_specs=(blocks, blocks),
        check_vma=False,
    )
```

```python
import math

import jax
import jax.numpy as jnp
import ml_dtypes
import numpy as np
from jax import lax
from jax.experimental import pallas as pl
from jax.experimental.pallas import tpu as pltpu
from jax.sharding import Mesh
from jax.sharding import PartitionSpec as P

C = 128
FF = 512
NX = 64
NY = 128
NZ = 128
MX = 16
MY = 32
MZ = 16
ROWS = 32
COLUMNS = 4
POINTS = NX * NY * NZ
KEPT = MX * MY * MZ
FORWARD_FACTOR = 1.0 / math.sqrt(POINTS)
INVERSE_FACTOR = 2.0 / math.sqrt(KEPT)
LOSS_SCALE = 0.5 * math.sqrt(KEPT / POINTS)
ROWS_A_STEP = 16
CHUNK = ROWS_A_STEP * NZ
CB = 64

GX = ("xl", "y", "z")
COL = ("xh", "co")
WIDE = ("y", "z", "xl", "xh")
F32 = jnp.float32
BF16 = jnp.bfloat16


def params(mebibytes=44):
    return pltpu.CompilerParams(dimension_semantics=("arbitrary",), vmem_limit_bytes=mebibytes * 1024 * 1024)


def signed(number):
    ladder = np.arange(number)
    return np.where(ladder < number // 2, ladder, ladder - number)


def angles(positions, frequencies, length):
    return (np.outer(positions, frequencies) % length) * (2.0 * math.pi / length)


def halves(table):
    high = table.astype(ml_dtypes.bfloat16)
    low = (table - high.astype(np.float64)).astype(ml_dtypes.bfloat16)
    return high, low


def wide(table):
    high, low = halves(table)
    return np.concatenate([high, high, low], axis=-1)


def tall(table):
    high, low = halves(table)
    return np.concatenate([high, low], axis=-2)


def rotation(positions, frequencies, length, sign):
    a = angles(positions, frequencies, length)
    c, s = np.cos(a), sign * np.sin(a)
    return np.stack([np.stack([c, -s]), np.stack([s, c])])


def back_order(column):
    order = []
    for part in range(4):
        xh, co = column // 2 ^ part % 2, column % 2 ^ part // 2
        order += [8 * zh + 4 * xh + 2 * co + m for zh in range(2) for m in range(2)]
    return np.array(order)


def out_order(core):
    order = []
    for part in range(2):
        for zh in range(2):
            for xh in range(2):
                order += [8 * zh + 4 * xh + 2 * (core ^ part) + m for m in range(2)]
    return np.array(order)


def z_tables():
    inverse, forward = [], []
    for column in range(COLUMNS):
        a = angles(np.arange(NZ), back_order(column), NZ)
        inverse.append(wide(np.stack([np.cos(a), -np.sin(a)], -1).reshape(NZ, 2 * MZ)))
    for core in range(2):
        a = angles(np.arange(NZ), out_order(core), NZ)
        high, low = halves(np.stack([np.cos(a), -np.sin(a)], -1).reshape(NZ, 2 * MZ).T)
        forward.append(np.block([[high, high], [low, np.zeros_like(low)]]))
    return np.stack(inverse), np.stack(forward)


def y_tables():
    inverse, forward = [], []
    for column in range(COLUMNS):
        rows = column * ROWS + np.arange(ROWS)
        r = rotation(rows, signed(MY), NY, 1.0)
        inverse.append(wide(r.transpose(0, 2, 1, 3).reshape(2 * ROWS, 2 * MY)))
        r = rotation(rows, signed(MY), NY, -1.0)
        forward.append(wide(r.transpose(0, 3, 1, 2).reshape(2 * MY, 2 * ROWS)))
    return np.stack(inverse), np.stack(forward)


def x_places():
    return np.arange(NX).reshape(2, 4, 8).transpose(1, 2, 0).reshape(NX)


def x_forward_table(fields, factor):
    r = rotation(x_places(), signed(MX), NX, -1.0) * factor
    t = np.zeros((fields, 2, MX, 2, NX, 2, 2, fields, 2))
    for s in range(fields):
        for m in range(2):
            for xh in range(2):
                t[s, :, :, m, :, xh, m, s, :] = r.transpose(0, 3, 2, 1)
    return tall(t.reshape(fields * 2 * MX * 2, NX * 2 * 2 * fields * 2))


def x_inverse_table(factor):
    r = rotation(x_places(), signed(MX), NX, 1.0) * factor
    t = np.zeros((NX, 2, 2, 2, 2, 2, MX, 2))
    for s in range(2):
        for m in range(2):
            t[:, m, s, :, s, :, :, m] = r.transpose(2, 0, 1, 3)
    return wide(t.reshape(NX * 8, 128))


def dot(a, b):
    return jnp.dot(a, b, preferred_element_type=F32)


def two(values):
    high = values.astype(BF16)
    return high, (values - high.astype(F32)).astype(BF16)


def three(values):
    high, low = two(values)
    return jnp.concatenate([high, low, high], axis=0)


def tall_dot(table, values):
    rows = table.shape[0] // 2
    high, low = two(values)
    first = dot(table, high)
    return first[:rows] + first[rows:] + dot(table[:rows], low)


def mode_rows(k, extra):
    zh, xh, m = k % 8 // 4, k % 4 // 2, k % 2
    return [pl.ds(zh * 32 + xl * 16 + xh * 8 + m * 4 + extra, 16, stride=64) for xl in range(2)]


def back_rows(k, extra):
    zh, m = k % 4 // 2, k % 2
    return [pl.ds(zh * 16 + xl * 8 + m * 4 + extra, 16, stride=32) for xl in range(2)]


def state_rows_of(k, extra):
    zh, xh, m = k % 8 // 4, k % 4 // 2, k % 2
    return [pl.ds(zh * 16 + xl * 8 + xh * 4 + m * 2 + extra, 16, stride=32) for xl in range(2)]


def rows_forward(values, fields, table, after, y):
    rows = dot(table, jnp.concatenate(two(values), axis=0))
    rows = rows[: 2 * MZ] + rows[2 * MZ :]
    start = pl.multiple_of(y * 2 * MZ, 2 * MZ)
    for s in range(fields):
        after[s, pl.ds(start, 2 * MZ), :] = rows[:, s * C : (s + 1) * C]


def columns_forward(fields, table, after, sink, half):
    pieces = [(k, s) for k in range(8 * half, 8 * half + 8) for s in range(fields)]
    for pair in zip(pieces[::2], pieces[1::2]):
        parts = []
        for k, s in pair:
            q = [after[s, pl.ds(2 * k + i, ROWS, stride=2 * MZ), :] for i in range(2)]
            parts.append(jnp.concatenate(q, axis=0))
        rows = dot(table, three(jnp.concatenate(parts, axis=1)))
        for i, (k, s) in enumerate(pair):
            for r in range(2):
                places = mode_rows(k, 2 * s + r) if fields == 2 else state_rows_of(k, r)
                for xl, place in enumerate(places):
                    at = r * MY + xl * 16
                    sink[place, :] = rows[at : at + 16, i * C : (i + 1) * C]


def kept_kernel(place, after, yf, keep):
    columns_forward(after.shape[0], yf[0], after, keep, 0)


def kept_stage(place, after, yf):
    shape = (512 * after.shape[0], C)
    return pl.pallas_call(
        kept_kernel,
        grid_spec=pltpu.PrefetchScalarGridSpec(
            num_scalar_prefetch=1,
            grid=(1,),
            in_specs=[still(after.shape), picked(yf, 0)],
            out_specs=still(shape),
        ),
        out_shape=jax.ShapeDtypeStruct(shape, F32),
        compiler_params=params(16),
    )(place, after, yf)


def state_kernel(place, state, zf, yf, keep, give, after):
    for y in range(0, ROWS, 2):
        pair = jnp.concatenate([state[(y + i) * NZ : (y + i + 1) * NZ] for i in range(2)], axis=1)
        rows = dot(zf[0, :, :NZ], pair)
        rows = rows[: 2 * MZ] + rows[2 * MZ :]
        for i in range(2):
            after[0, pl.ds((y + i) * 2 * MZ, 2 * MZ), :] = rows[:, i * C : (i + 1) * C]
    columns_forward(1, yf[0], after, keep, 0)
    columns_forward(1, yf[0], after, give, 1)


def ready_kernel(place, w1_, w2_, yi_, zi_, zf_, yf_, w1, w2, w1t, w2t, yi, zi, zf, yf):
    w1[...] = w1_[...]
    w2[...] = w2_[...]
    w1t[...] = w1_[...].T
    w2t[...] = w2_[...].T
    yi[...] = yi_[0]
    zi[...] = zi_[0]
    zf[...] = zf_[0]
    yf[...] = yf_[0]


def y_inverse(parts, table, half):
    for k in range(4 * len(parts)):
        rows = []
        for s in range(2):
            p = [parts[k // 4][place, :] for i in range(2) for place in back_rows(k, 2 * s + i)]
            rows.append(jnp.concatenate(p, axis=0))
        rows = dot(table, three(jnp.concatenate(rows, axis=1)))
        for s in range(2):
            half[s, pl.ds(k * 64, 64), :] = rows[:, s * C : (s + 1) * C]


def early_kernel(q00, q10, q01, yi, half):
    y_inverse((q00, q10, q01), yi[...], half)


def field_kernel(
    early, q11, state, target, w1, w2, w1t, w2t, yi, zi, zf, yf, after, give, late
):
    step = pl.program_id(0)

    @pl.when(step == 0)
    def _():
        y_inverse((q11,), yi[...], late)

    first = step * ROWS_A_STEP
    fields = []
    for i in range(ROWS_A_STEP):
        taken = []
        for part, count in ((early, 24), (late, 8)):
            taken.append(jnp.concatenate([part[s, pl.ds(first + i, count, stride=ROWS), :] for s in range(2)], axis=1))
        fields.append(dot(zi[...], three(jnp.concatenate(taken, axis=0))))
    fields = jnp.concatenate(fields, axis=0).astype(BF16)
    primal, tangent = fields[:, :C], fields[:, C:]
    layer_input = state[...].astype(F32) + primal.astype(F32)
    hidden = dot(layer_input.astype(BF16), w1[...])
    mass = 0.5 * (1.0 + lax.erf(hidden * math.sqrt(0.5)))
    density = jnp.exp(-0.5 * hidden * hidden) * (1.0 / math.sqrt(2.0 * math.pi))
    slope = mass + hidden * density
    activation = (hidden * mass).astype(BF16)
    seed_primal = LOSS_SCALE * (layer_input + dot(activation, w2[...]) - target[...].astype(F32))
    hidden_tangent = dot(tangent, w1[...])
    activation_tangent = (slope * hidden_tangent).astype(BF16)
    seed_tangent = LOSS_SCALE * (tangent.astype(F32) + dot(activation_tangent, w2[...]))
    back_primal = dot(seed_primal.astype(BF16), w2t[...])
    back_tangent = dot(seed_tangent.astype(BF16), w2t[...])
    delta_primal = (slope * back_primal).astype(BF16)
    bend = density * (2.0 - hidden * hidden)
    delta_tangent = (bend * hidden_tangent * back_primal + slope * back_tangent).astype(BF16)
    cotangents = [seed_primal + dot(delta_primal, w1t[...]), seed_tangent + dot(delta_tangent, w1t[...])]
    cotangents = jnp.concatenate(cotangents, axis=1)
    for i in range(ROWS_A_STEP):
        rows_forward(cotangents[i * NZ : (i + 1) * NZ], 2, zf[...], after, first + i)

    @pl.when(step == ROWS // ROWS_A_STEP - 1)
    def _():
        columns_forward(2, yf[...], after, give, 1)


def whole(shape):
    return pl.BlockSpec(shape, lambda i: (0,) * len(shape))


def still(shape):
    return pl.BlockSpec(shape, lambda i, place: (0,) * len(shape))


def picked(table, index):
    return pl.BlockSpec((1,) + table.shape[1:], lambda i, place: (place[index], 0, 0))


def state_stage(place, state, zf, yf):
    shape = jax.ShapeDtypeStruct((512, C), F32)
    return pl.pallas_call(
        state_kernel,
        grid_spec=pltpu.PrefetchScalarGridSpec(
            num_scalar_prefetch=1,
            grid=(1,),
            in_specs=[still(state.shape), picked(zf, 1), picked(yf, 0)],
            out_specs=(still((512, C)), still((512, C))),
            scratch_shapes=[pltpu.VMEM((1, 1024, C), F32)],
        ),
        out_shape=(shape, shape),
        compiler_params=params(),
    )(place, state, zf, yf)


def ready_stage(place, w1, w2, tables):
    shapes = [(C, FF), (FF, C), (FF, C), (C, FF)] + [t.shape[1:] for t in tables]
    return pl.pallas_call(
        ready_kernel,
        grid_spec=pltpu.PrefetchScalarGridSpec(
            num_scalar_prefetch=1,
            grid=(1,),
            in_specs=[still(w1.shape), still(w2.shape)] + [picked(t, i) for t, i in zip(tables, (0, 0, 1, 0))],
            out_specs=tuple(still(shape) for shape in shapes),
        ),
        out_shape=tuple(jax.ShapeDtypeStruct(shape, BF16) for shape in shapes),
        compiler_params=params(16),
    )(place, w1, w2, *tables)


def early_stage(q00, q10, q01, yi):
    shape = (2, 768, C)
    return pl.pallas_call(
        early_kernel,
        grid=(1,),
        in_specs=[whole((512, C))] * 3 + [whole(yi.shape)],
        out_specs=whole(shape),
        out_shape=jax.ShapeDtypeStruct(shape, F32),
        compiler_params=params(16),
    )(q00, q10, q01, yi)


def field_stage(early, q11, state, target, ready):
    moving = pl.BlockSpec((CHUNK, C), lambda i: (i, 0))
    shapes = (2, 1024, C), (1024, C)
    return pl.pallas_call(
        field_kernel,
        grid=(ROWS // ROWS_A_STEP,),
        in_specs=[whole(early.shape), whole((512, C))] + [moving] * 2 + [whole(r.shape) for r in ready],
        out_specs=tuple(whole(shape) for shape in shapes),
        out_shape=tuple(jax.ShapeDtypeStruct(shape, F32) for shape in shapes),
        scratch_shapes=[pltpu.VMEM((2, 256, C), F32)],
        compiler_params=params(),
    )(early, q11, state, target, *ready)


def mix_kernel(received, weight, direction, xf, xi_, spectra, planes, total, xi, arrival):
    step = pl.program_id(0)
    second = pltpu.make_async_copy(xi_, xi, arrival)

    @pl.when(step == 0)
    def _():
        second.start()
        spectra[...] = tall_dot(xf[...], received[...])
        total[...] = jnp.zeros_like(total)

    turned = pltpu.roll(spectra[...], C - step * CB, 1)
    sums = [total[i] for i in range(4)]
    for j in range(CB):
        column = jnp.broadcast_to(turned[:, j : j + 1], (64, C))
        real, imag = column[:32], column[32:]
        for s, w in ((0, weight), (1, direction)):
            wr, wi = w[0, j].astype(F32), w[1, j].astype(F32)
            sums[2 * s] = sums[2 * s] + (wr * real - wi * imag)
            sums[2 * s + 1] = sums[2 * s + 1] + (wr * imag + wi * real)
    for i in range(4):
        total[i] = sums[i]

    @pl.when(step == C // CB - 1)
    def _():
        second.wait()
        out = dot(xi[...], three(jnp.concatenate(sums, axis=0)))
        planes[...] = out


def mix_stage(received, weight, direction):
    xf = x_forward_table(1, FORWARD_FACTOR)
    xi = x_inverse_table(INVERSE_FACTOR)
    weight = weight.reshape(2, C, 32, C)
    direction = direction.reshape(2, C, 32, C)
    moving = pl.BlockSpec((2, CB, 32, C), lambda i: (0, i, 0, 0))
    return pl.pallas_call(
        mix_kernel,
        grid=(C // CB,),
        in_specs=[whole(received.shape), moving, moving, whole(xf.shape), pl.BlockSpec(memory_space=pltpu.HBM)],
        out_specs=(whole((64, C)), whole((NX * 8, C))),
        out_shape=(jax.ShapeDtypeStruct((64, C), F32), jax.ShapeDtypeStruct((NX * 8, C), F32)),
        scratch_shapes=[
            pltpu.VMEM((4, 32, C), F32),
            pltpu.VMEM(xi.shape, BF16),
            pltpu.SemaphoreType.DMA,
        ],
        compiler_params=params(),
    )(received, weight, direction, jnp.asarray(xf), pltpu.with_memory_space_constraint(jnp.asarray(xi), pltpu.HBM))


def outer_kernel(received, spectra, xf, gradient, curvature, adjoint):
    step = pl.program_id(0)

    @pl.when(step == 0)
    def _():
        adjoint[...] = tall_dot(xf[...], received[...])

    turned = pltpu.roll(spectra[...], C - step * CB, 1)
    pieces = [adjoint[32 * i : 32 * i + 32, :] for i in range(4)]
    for j in range(CB):
        column = jnp.broadcast_to(turned[:, j : j + 1], (64, C))
        real, imag = column[:32], column[32:]
        for s, sink in ((0, gradient), (1, curvature)):
            re, im = pieces[2 * s], pieces[2 * s + 1]
            sink[0, j] = (real * re + imag * im).astype(BF16)
            sink[1, j] = (real * im - imag * re).astype(BF16)


def outer_stage(received, spectra):
    xf = x_forward_table(2, INVERSE_FACTOR)
    moving = pl.BlockSpec((2, CB, 32, C), lambda i: (0, i, 0, 0))
    shape = jax.ShapeDtypeStruct((2, C, 32, C), BF16)
    return pl.pallas_call(
        outer_kernel,
        grid=(C // CB,),
        in_specs=[whole(received.shape), whole(spectra.shape), whole(xf.shape)],
        out_specs=(moving, moving),
        out_shape=(shape, shape),
        scratch_shapes=[pltpu.VMEM((128, C), F32)],
        compiler_params=params(),
    )(received, spectra, jnp.asarray(xf))


def exchange(rows, group):
    size = lax.axis_size(group)
    return lax.all_to_all(rows.reshape(size, -1, C), group, 0, 0, tiled=True).reshape(rows.shape)


def swap(rows, axis):
    return lax.ppermute(rows, axis, [(0, 1), (1, 0)])


def local(state, target, spectral_weight, direction_weight, inner_weight, outer_weight):
    place = jnp.stack([lax.axis_index(COL), lax.axis_index("co")]).astype(jnp.int32)
    yi, yf = (jnp.asarray(t) for t in y_tables())
    zi, zf = (jnp.asarray(t) for t in z_tables())

    def rows_of(cells):
        return cells[:, 0].transpose(1, 2, 0).reshape(ROWS * NZ, C)

    state_rows = rows_of(state)
    keep, give = state_stage(place, state_rows, zf, yf)
    received = exchange(keep + swap(give, "co"), WIDE)
    spectra, planes = mix_stage(received, spectral_weight, direction_weight)
    q00 = exchange(planes, WIDE[:3])
    q10 = swap(q00, "xh")
    q01 = swap(q00, "co")
    q00, target, w1, w2 = lax.optimization_barrier((q00, target, inner_weight, outer_weight))
    ready = ready_stage(place, w1, w2, (yi, zi, zf, yf))
    target_rows = rows_of(target)
    q10, ready, target_rows = lax.optimization_barrier((q10, ready, target_rows))
    q11 = swap(q10, "co")
    early = early_stage(q00, q10, q01, ready[4])
    after, give = field_stage(early, q11, state_rows, target_rows, ready)
    adjoint = exchange(swap(give, "co") + kept_stage(0 * place, after, ready[7][None]), WIDE)
    gradient, curvature = outer_stage(adjoint, spectra)
    shape = (2, C, MX, 2, C)
    return gradient.reshape(shape), curvature.reshape(shape)


def solution(mesh):
    fine = Mesh(mesh.devices.reshape(2, 4, 8, 2, 2), GX + COL)
    grid = P(None, GX, COL, None)
    blocks = P(None, None, None, GX + COL, None)
    return jax.shard_map(
        local,
        mesh=fine,
        in_specs=(grid, grid, blocks, blocks, P(), P()),
        out_specs=(blocks, blocks),
        check_vma=False,
    )
```
